512 devices in a mesh: segment: 4 (over x_hi, core), lat: 128 (over z, y, x_lo).
Axes of the slice: x: 4 (x_hi: 2, x_lo: 2; x = x_hi * 2 + x_lo), y: 8, z: 8, core: 2. Of those that a mesh axis runs over, the one named last changes fastest.
Arguments:
- fields: bfloat16 [4, 21504, 144], P('segment', 'lat'), may hold values from -6 to 6
- band_rows: int32 [128], replicated, may hold values from 1 to 2, 192 in all
- window_table: int32 [128], replicated, may hold values from -1 to 118, as said below
- level_embed: bfloat16 [2, 1024], replicated, may hold values from -6 to 6
- embed_weight: bfloat16 [144, 1024], replicated, may hold values from -0.5 to 0.5
- attn_weight: bfloat16 [4, 1024, 4096], P('segment', None, 'lat'), may hold values from -0.1875 to 0.1875
- norm_gain: float32 [4, 1024], P('segment'), may hold values from 0.5 to 1.5
- head_weight: bfloat16 [1024, 144], replicated, may hold values from -0.1875 to 0.1875
Outputs:
- decoded: bfloat16 [4, 21504, 144], P('segment', 'lat')
- window_decoded: bfloat16 [4, 18432, 144], P('segment', 'lat')
The draws below stay inside these ranges and needn't reach their ends.
Inputs may be any that keep to these rules, and one draw needn't show every extreme that they name: `window_table`: each window 0 to 118 appears once, other shards hold -1. `band_rows`: rows of each band sum to 192.
All inputs are finite; a program needn't handle non-finite values.
Results may differ from the reference program's by a relative error of at most 0.025.
Values may be sent and summed in bfloat16 or wider, within the bound.
No kernel may reach another device: no remote copies, remote signals or barrier semaphores. Data moves between devices by JAX's collectives and lax.ppermute only.
A program may use at most 64 MiB of HBM per device.

```python
import math
import jax
import jax.numpy as jnp
import numpy as np
from jax import lax

D = 1024
HEAD_DIM = 64
FEAT = 144
LEV = 2
WIN_ROWS = 12
WIN_COLS = 6
LW = 7
SLABS = 4
WTOK = 144
BAND_TOK = 168
N_SEGMENT = 4
N_LAT = 128


def draw_window_table(key, part):
    order = jax.random.permutation(key, N_LAT).astype(jnp.int32)
    count = (N_LAT // 8 + 1) * LW
    return jnp.where(order < count, order, -1).astype(jnp.int32)


def level_of(stream_key, dims, shards, smallest, largest):
    def one(dim, parts):
        steps = jax.random.uniform(jax.random.fold_in(jax.random.fold_in(stream_key, 6), dim), (parts,), jnp.float32, smallest / len(shards), largest / len(shards))
        return jnp.repeat(jnp.exp(steps), dims[dim] // parts).reshape((-1,) + (1,) * (len(dims) - dim - 1))

    level = one(*shards[0])
    for cut in shards[1:]:
        level = level * one(*cut)
    return level


def profile(count, total, bound, slope):
    weights = [(1 << 20) // math.isqrt(rank ** slope) + 1 for rank in range(2, count + 1)]
    surplus, counts = total - bound - (count - 1), [1] * (count - 1)
    while surplus > 0:
        free = [i for i in range(count - 1) if counts[i] < bound]
        whole, budget = sum([weights[i] for i in free]), surplus
        for i in free:
            more = min(bound - counts[i], max(1, budget * weights[i] // whole), surplus)
            counts[i] = counts[i] + more
            surplus = surplus - more
    return np.array([bound] + counts)


def ragged_sizes(own_key, count, total, bound, skew):
    if count == 2:
        one = jax.random.randint(own_key, (), max(1, total - bound), min(bound, total - 1) + 1)
        return jnp.stack([one, total - one])
    lengths = jnp.asarray(profile(count, total, bound, skew), jnp.int32)
    twos = (count - 1) // 2
    giver, taker = lengths[1:1 + 2 * twos:2], lengths[2:2 + 2 * twos:2]
    room = jnp.minimum(giver - 1, bound - taker)
    passed = jax.random.randint(jax.random.fold_in(own_key, 1), (twos,), 0, 1 << 20) % (room + 1)
    lengths = lengths.at[1:1 + 2 * twos:2].set(giver - passed).at[2:2 + 2 * twos:2].set(taker + passed)
    return lengths[jax.random.permutation(jax.random.fold_in(own_key, 2), count)]


def noise(key, extent, spread, limit, split=(), kind=jnp.bfloat16):
    values = spread * jax.random.normal(key, extent, jnp.float32)
    if split:
        values = values * level_of(key, extent, split, -0.22, 0.18)
    return jnp.clip(values, -limit, limit).astype(kind)


def setup_inputs(seed: int = 0) -> dict:
    arg_keys = jax.random.split(jax.random.key(seed), 9)
    return {
        "fields": noise(arg_keys[0], (SLABS, N_LAT * BAND_TOK, FEAT), 1.0, 6.0, ((0, 4), (1, 128))),
        "band_rows": ragged_sizes(arg_keys[1], N_LAT, 3 * N_LAT // 2, 2, 0).astype(jnp.int32),
        "window_table": draw_window_table(jax.random.fold_in(arg_keys[8], 71), 0),
        "level_embed": noise(arg_keys[3], (LEV, D), 1.0, 6.0),
        "embed_weight": noise(arg_keys[4], (FEAT, D), FEAT ** -0.5, 0.5),
        "attn_weight": noise(arg_keys[5], (N_SEGMENT, D, 4 * D), D ** -0.5, 0.1875, ((0, 4), (2, 128))),
        "norm_gain": jnp.clip(1.0 + 0.1 * jax.random.normal(arg_keys[6], (N_SEGMENT, D), jnp.float32), 0.5, 1.5),
        "head_weight": noise(arg_keys[7], (D, FEAT), D ** -0.5, 0.1875),
    }


def attend_block(tokens, gain, weight, allowed):
    width = tokens.shape[-1]
    heads = width // HEAD_DIM
    wide = tokens.astype(jnp.float32)
    normed = (wide * lax.rsqrt(lax.optimization_barrier(jnp.mean(wide * wide, axis=-1, keepdims=True)) + 1e-06) * gain).astype(jnp.bfloat16)
    project = jnp.dot(normed, weight[:, :3 * width], preferred_element_type=jnp.float32).astype(jnp.bfloat16)
    query = project[:, :width].reshape(-1, heads, HEAD_DIM).astype(jnp.float32)
    keyed = project[:, width:2 * width].reshape(-1, heads, HEAD_DIM).astype(jnp.float32)
    valued = project[:, 2 * width:].reshape(-1, heads, HEAD_DIM).astype(jnp.float32)
    scores = jnp.einsum('qhd,khd->hqk', query, keyed) / math.sqrt(HEAD_DIM)
    scores = jnp.where(allowed[None], scores, -1e+30)
    probs = jax.nn.softmax(scores, axis=-1).astype(jnp.bfloat16)
    mixed = jnp.einsum('hqk,khd->qhd', probs.astype(jnp.float32), valued).astype(jnp.bfloat16).reshape(-1, width)
    update = jnp.dot(mixed, weight[:, 3 * width:], preferred_element_type=jnp.float32)
    return (wide + update).astype(jnp.bfloat16)

def reference(fields, band_rows, window_table, level_embed, embed_weight, attn_weight, norm_gain, head_weight):
    total_rows = 3 * N_LAT // 2
    windows = (total_rows // WIN_ROWS + 1) * LW
    lon_cells = WIN_COLS * LW
    row_ends = jnp.cumsum(band_rows).astype(jnp.int32)
    row_starts = (row_ends - band_rows).astype(jnp.int32)
    token = jnp.arange(WTOK, dtype=jnp.int32)
    level = token // (WIN_ROWS * WIN_COLS)
    lat_off = token // WIN_COLS % WIN_ROWS
    lon_off = token % WIN_COLS
    window = jnp.arange(windows, dtype=jnp.int32)[:, None]
    grid_row = WIN_ROWS * (window // LW) - WIN_ROWS // 2 + lat_off[None]
    inside = (grid_row >= 0) & (grid_row < total_rows)
    band = lax.optimization_barrier(jnp.sum((row_ends[None, None, :] <= grid_row[..., None]).astype(jnp.int32), axis=-1))
    band = jnp.clip(band, 0, N_LAT - 1).astype(jnp.int32)
    local_row = grid_row - row_starts[band]
    column = WIN_COLS * (window % LW) + lon_off[None]
    source = band * BAND_TOK + (local_row * lon_cells + column) * LEV + level[None]
    source = jnp.where(inside, source, 0).astype(jnp.int32)
    same_column = (lat_off[:, None] == lat_off[None, :]) & (lon_off[:, None] == lon_off[None, :])
    level_rows = jnp.broadcast_to(level_embed.astype(jnp.float32)[:, None, :], (LEV, WIN_ROWS * WIN_COLS, level_embed.shape[1])).reshape(WTOK, -1)

    def one_slab(slab_fields):

        def one_window(operand):
            picks, keep = operand
            raw_tokens = jnp.take(slab_fields, picks, axis=0) * keep[:, None].astype(jnp.bfloat16)
            hidden = (jnp.dot(raw_tokens, embed_weight, preferred_element_type=jnp.float32) + level_rows).astype(jnp.bfloat16)
            window_keys = jnp.broadcast_to(keep[None, :], (WTOK, WTOK))
            hidden = attend_block(hidden, norm_gain[0], attn_weight[0], same_column)
            hidden = attend_block(hidden, norm_gain[1], attn_weight[1], window_keys)
            hidden = attend_block(hidden, norm_gain[2], attn_weight[2], window_keys)
            hidden = attend_block(hidden, norm_gain[3], attn_weight[3], same_column)
            result = jnp.dot(hidden, head_weight, preferred_element_type=jnp.float32) * keep[:, None].astype(jnp.float32)
            return result.astype(jnp.bfloat16)
        return lax.map(one_window, (source, inside))
    results = lax.map(one_slab, fields)
    held = jnp.clip(window_table, 0, windows - 1).astype(jnp.int32)
    window_decoded = results[:, held] * (window_table >= 0)[None, :, None, None].astype(jnp.bfloat16)
    window_decoded = window_decoded.reshape(SLABS, N_LAT * WTOK, -1)
    slot = jnp.arange(BAND_TOK, dtype=jnp.int32)
    slot_row = slot // (lon_cells * LEV)
    slot_col = slot // LEV % lon_cells
    slot_lev = slot % LEV
    present = slot_row[None] < band_rows[:, None]
    band_grid = row_starts[:, None] + slot_row[None]
    window_row = (band_grid + WIN_ROWS // 2) // WIN_ROWS
    lat_in = band_grid + WIN_ROWS // 2 - WIN_ROWS * window_row
    window_id = jnp.where(present, window_row * LW + slot_col[None] // WIN_COLS, 0).astype(jnp.int32)
    token_id = jnp.where(present, (slot_lev[None] * WIN_ROWS + lat_in) * WIN_COLS + slot_col[None] % WIN_COLS, 0).astype(jnp.int32)
    decoded = results[:, window_id, token_id] * present[None, :, :, None].astype(jnp.bfloat16)
    return (decoded.reshape(SLABS, N_LAT * BAND_TOK, -1), window_decoded)
```

```python
import functools
import math

import jax
import jax.numpy as jnp
from jax import lax
from jax.experimental import pallas as pl
from jax.experimental.pallas import tpu as pltpu
from jax.sharding import Mesh
from jax.sharding import PartitionSpec as P

HEAD_DIM = 64
LEV = 2
WIN_ROWS = 12
WIN_COLS = 6
WTOK = 144
FEAT = 144
LW = 7
PIECE = WIN_COLS * LEV * FEAT
PACK = 16
BF = jnp.bfloat16
F32 = jnp.float32
LAT = ("z", "y", "xl")
DOUBLING = (4, 2, 1)
OFFS = (0, 4, 2, 6, 1, 5, 3, 7)
MIB = 1 << 20

VMEM = pl.BlockSpec(memory_space=pltpu.VMEM)
SMEM = pl.BlockSpec(memory_space=pltpu.SMEM)
ANY = pl.BlockSpec(memory_space=pl.ANY)


def ring(value, axis, by):
    n = lax.axis_size(axis)
    return lax.ppermute(value, axis, [(i, (i + by) % n) for i in range(n)])


def swap(value, axis, bit):
    n = lax.axis_size(axis)
    return lax.ppermute(value, axis, [(i, i ^ bit) for i in range(n)])


def pack_kernel(table, rows_ref, out_ref):
    @pl.loop(0, table.shape[0])
    def _(j):
        column = lax.rem(jnp.maximum(table[j], 0), LW)
        out_ref[2 * j] = rows_ref[column]
        out_ref[2 * j + 1] = rows_ref[LW + column]


def pick_kernel(where, bands, table, came_ref, out_ref):
    window = table[where[0]]
    first = WIN_ROWS * lax.div(jnp.maximum(window, 0), LW) - WIN_ROWS // 2
    out_ref[...] = jnp.zeros_like(out_ref)

    def band(i, start):
        row = start - first
        count = bands[i]

        @pl.when((window >= 0) & (row >= 0) & (row < WIN_ROWS))
        def _():
            out_ref[row] = came_ref[2 * i]

        @pl.when((window >= 0) & (count > 1) & (row >= -1) & (row < WIN_ROWS - 1))
        def _():
            out_ref[row + 1] = came_ref[2 * i + 1]

        return start + count

    lax.fori_loop(0, bands.shape[0], band, jnp.int32(0))


def unpick_kernel(where, bands, table, rows_ref, out_ref):
    window = table[where[0]]
    first = WIN_ROWS * lax.div(jnp.maximum(window, 0), LW) - WIN_ROWS // 2

    def band(i, start):
        row = start - first
        out_ref[2 * i] = rows_ref[jnp.clip(row, 0, WIN_ROWS - 1)]
        out_ref[2 * i + 1] = rows_ref[jnp.clip(row + 1, 0, WIN_ROWS - 1)]
        return start + bands[i]

    lax.fori_loop(0, bands.shape[0], band, jnp.int32(0))


def unpack_kernel(where, bands, table, came_ref, out_ref):
    mine = where[0]
    start = lax.fori_loop(0, mine, lambda i, total: total + bands[i], jnp.int32(0))
    count = bands[mine]
    wide = lax.div(start + WIN_ROWS // 2, WIN_ROWS)
    wide_next = lax.div(start + 1 + WIN_ROWS // 2, WIN_ROWS)
    out_ref[...] = jnp.zeros_like(out_ref)

    @pl.loop(0, table.shape[0])
    def _(j):
        window = table[j]
        across = lax.div(jnp.maximum(window, 0), LW)
        column = lax.rem(jnp.maximum(window, 0), LW)

        @pl.when((window >= 0) & (across == wide))
        def _():
            out_ref[column] = came_ref[2 * j]

        @pl.when((window >= 0) & (count > 1) & (across == wide_next))
        def _():
            out_ref[LW + column] = came_ref[2 * j + 1]


def to_rows(tokens):
    rows = tokens.reshape(-1, PIECE)
    return jnp.pad(rows, ((0, 0), (0, PACK * 128 - PIECE))).reshape(-1, PACK, 128)


def from_rows(rows):
    return rows.reshape(-1, PACK * 128)[:, :PIECE].reshape(-1, FEAT)


def join_kernel(pos, *refs):
    out, sem = refs[-2], refs[-1]
    pieces = refs[:-2]
    half = len(pieces) // 2
    z, y = pos[1], pos[2]

    def copies(side, index):
        ref = pieces[side * half + index]
        step = (0, -1, -2, -3, 1, 2, 3, 4, 4)[index]
        subs = range(8) if index < 7 else (range(4) if index == 7 else range(4, 8))
        for slot, sub in enumerate(subs):
            if side == 0:
                plane, line = lax.rem(z + step + 8, 8), y ^ OFFS[sub]
            else:
                plane, line = z ^ OFFS[sub], lax.rem(y + step + 8, 8)
            row = pl.multiple_of((plane * 8 + line) * 64, 64)
            yield pltpu.make_async_copy(
                ref.at[pl.ds(slot * 64, 64)], out.at[side, pl.ds(row, 64)], sem
            )

    every = [c for side in range(2) for i in range(half) for c in copies(side, i)]
    for c in every:
        c.start()
    for c in every:
        c.wait()


def gather_section(weight, pos):
    mine = weight[0].T
    pair = lax.all_gather(mine, "xl", axis=0, tiled=True)
    a, b = pair[:, :512], pair[:, 512:]
    for bit in DOUBLING:
        a_far, b_far = swap(a, "y", bit), swap(b, "z", bit)
        a, b = jnp.concatenate([a, a_far]), jnp.concatenate([b, b_far])
    pieces = []
    chains = [(a, "z", 1), (a, "z", -1), (b, "y", 1), (b, "y", -1)]
    got = [[] for _ in chains]
    held = [c[0] for c in chains]
    for step in range(4):
        for n, (_, axis, by) in enumerate(chains):
            value = held[n]
            if step == 3:
                value = value[:256] if by > 0 else value[256:]
            held[n] = ring(value, axis, by)
            got[n].append(held[n])
    for own, ahead, behind in ((a, got[0], got[1]), (b, got[2], got[3])):
        pieces += [own, *ahead[:3], *behind[:3], ahead[3], behind[3]]
    return pl.pallas_call(
        join_kernel,
        out_shape=jax.ShapeDtypeStruct((2, 4096, 512), BF),
        in_specs=[SMEM] + [ANY] * len(pieces),
        out_specs=ANY,
        scratch_shapes=[pltpu.SemaphoreType.DMA(())],
        name="join",
    )(pos, *pieces)


def matmul_t(left, right):
    return lax.dot_general(left, right, (((1,), (1,)), ((), ())), preferred_element_type=F32)


def block(hidden, gain, weights, wait, allowed):
    wide = hidden.astype(F32)
    scale = lax.rsqrt(jnp.mean(wide * wide, axis=-1, keepdims=True) + 1e-06)
    normed = (wide * scale * gain).astype(BF)

    def project(left, part):
        wait(part)
        rows = slice(1024 * part, 1024 * (part + 1))
        return matmul_t(left[:, :512], weights[0, rows]) + matmul_t(left[:, 512:], weights[1, rows])

    query = (project(normed, 0).astype(BF).astype(F32) * (1 / math.sqrt(HEAD_DIM))).astype(BF)
    keyed = project(normed, 1).astype(BF)
    valued = project(normed, 2).astype(BF)
    low = lax.broadcasted_iota(jnp.int32, (WTOK, 128), 1) < HEAD_DIM
    slabs = hidden.shape[0] // WTOK
    all_mixed = []
    for slab in range(slabs):
        here = slice(WTOK * slab, WTOK * (slab + 1))
        mixed = []
        for two in range(8):
            lanes = slice(128 * two, 128 * (two + 1))
            q2, k2, v2 = query[here, lanes], keyed[here, lanes], valued[here, lanes]
            outs = []
            for part in range(2):
                q1 = jnp.where(low if part == 0 else ~low, q2, jnp.zeros_like(q2))
                scores = jnp.where(allowed, matmul_t(q1, k2), -1e30)
                top = jnp.max(scores, axis=-1, keepdims=True)
                grown = jnp.exp(scores - top)
                probs = (grown / jnp.sum(grown, axis=-1, keepdims=True)).astype(BF)
                outs.append(jnp.dot(probs, v2, preferred_element_type=F32))
            mixed.append(jnp.where(low, outs[0], outs[1]).astype(BF))
        all_mixed.append(jnp.concatenate(mixed, axis=1))
    mixed = jnp.concatenate(all_mixed, axis=0) if slabs > 1 else all_mixed[0]
    return (wide + project(mixed, 3)).astype(BF)


def sections_kernel(
    pos, bands, table, raw_ref, came_ref, embed_ref, level_ref, gain_ref, head_ref, own_ref, other_ref,
    hidden_ref, out_ref, rows_ref, weights, sems,
):
    core, late = pos[3], pos[4]

    def load(source, section):
        for part in range(4):
            rows = pl.ds(1024 * part, 1024)
            pltpu.make_async_copy(
                source.at[:, rows], weights.at[section, :, rows], sems.at[section, part]
            ).start()

    @pl.when(core == 0)
    def _():
        load(own_ref, 0)
        load(other_ref, 1)

    @pl.when(core == 1)
    def _():
        load(other_ref, 0)
        load(own_ref, 1)

    def waiter(section):
        def wait(part):
            rows = pl.ds(1024 * part, 1024)
            pltpu.make_async_copy(
                own_ref.at[:, rows], weights.at[section, :, rows], sems.at[section, part]
            ).wait()

        return wait

    slabs = raw_ref.shape[0]
    query_token = lax.broadcasted_iota(jnp.int32, (WTOK, WTOK), 0)
    key_token = lax.broadcasted_iota(jnp.int32, (WTOK, WTOK), 1)
    half = WIN_ROWS * WIN_COLS
    same = lax.rem(query_token, half) == lax.rem(key_token, half)
    window = table[pos[0]]
    first = WIN_ROWS * lax.div(jnp.maximum(window, 0), LW) - WIN_ROWS // 2
    total_rows = 3 * bands.shape[0] // 2

    def inside(token):
        row = first + lax.rem(lax.div(token, WIN_COLS), WIN_ROWS)
        return (window >= 0) & (row >= 0) & (row < total_rows)

    keep = inside(key_token)
    is_late = late == 1
    first_mask = (same & (late == 0)) | (keep & (late == 1))
    second_mask = (keep & (late == 0)) | (same & (late == 1))
    to_window = (lax.div(query_token, half) == lax.rem(key_token, LEV)) & (
        lax.rem(query_token, half) == lax.div(key_token, LEV)
    )
    from_window = (lax.rem(query_token, LEV) == lax.div(key_token, half)) & (
        lax.div(query_token, LEV) == lax.rem(key_token, half)
    )
    to_window = to_window.astype(BF)
    from_window = from_window.astype(BF)
    upper = lax.broadcasted_iota(jnp.int32, (WTOK, 1), 0) < half
    level_rows = jnp.where(upper, level_ref[0:1].astype(F32), level_ref[1:2].astype(F32))
    starts = []
    for slab in range(slabs):
        raw = jnp.dot(to_window, raw_ref[slab], preferred_element_type=F32).astype(BF)
        embedded = (jnp.dot(raw, embed_ref[...], preferred_element_type=F32) + level_rows).astype(BF)
        starts.append(jnp.where(is_late, came_ref[slab], embedded))
    hidden = jnp.concatenate(starts, axis=0) if slabs > 1 else starts[0]
    hidden = block(hidden, gain_ref[0:1], weights.at[0], waiter(0), first_mask)
    hidden = block(hidden, gain_ref[1:2], weights.at[1], waiter(1), second_mask)
    result = jnp.dot(hidden, head_ref[...], preferred_element_type=F32)
    keep_row = inside(lax.broadcasted_iota(jnp.int32, (WTOK, 1), 0))
    for slab in range(slabs):
        here = slice(WTOK * slab, WTOK * (slab + 1))
        hidden_ref[slab] = hidden[here]
        out = jnp.where(keep_row, result[here], 0.0).astype(BF)
        out_ref[slab] = out
        rows_ref[slab] = jnp.dot(from_window, out, preferred_element_type=F32).astype(BF)


def two_sections(pos, bands, table, raw, came, embed, level, gains, head, own, other):
    slabs = raw.shape[0]
    width = embed.shape[1]
    return pl.pallas_call(
        sections_kernel,
        out_shape=(
            jax.ShapeDtypeStruct((slabs, WTOK, width), BF),
            jax.ShapeDtypeStruct((slabs, WTOK, FEAT), BF),
            jax.ShapeDtypeStruct((slabs, WTOK, FEAT), BF),
        ),
        in_specs=[SMEM] * 3 + [VMEM] * 6 + [ANY] * 2,
        out_specs=(VMEM,) * 3,
        scratch_shapes=[
            pltpu.VMEM((2, 2, 4096, 512), BF),
            pltpu.SemaphoreType.DMA((2, 4)),
        ],
        compiler_params=pltpu.CompilerParams(vmem_limit_bytes=48 * MIB),
        name="sections",
    )(pos, bands, table, raw, came, embed, level, gains, head, own, other)


def small_call(body, out_rows, scalars, value, name):
    return pl.pallas_call(
        body,
        out_shape=jax.ShapeDtypeStruct((out_rows, PACK, 128), BF),
        in_specs=[SMEM] * len(scalars) + [VMEM],
        out_specs=VMEM,
        name=name,
    )(*scalars, value)


def per_device(
    fields, band_rows, window_table, level_embed, embed_weight, attn_weight, norm_gain, head_weight
):
    late, core = lax.axis_index("xh"), lax.axis_index("c")
    pos = jnp.stack([lax.axis_index(LAT), lax.axis_index("z"), lax.axis_index("y"), core, late])
    scalars = (pos, band_rows, window_table)
    lat_count = band_rows.shape[0]
    is_late = late == 1

    message = small_call(pack_kernel, 2 * lat_count, (window_table,), to_rows(fields[0]), "pack")
    arrived = lax.all_to_all(message, LAT, 0, 0, tiled=True)
    raw_rows = small_call(pick_kernel, WIN_ROWS, scalars, arrived, "pick")
    own_raw = from_rows(raw_rows)
    far_raw = swap(own_raw, "xh", 1)

    own = gather_section(attn_weight, pos)
    other = swap(own, "c", 1)
    gains = lax.all_gather(norm_gain, "c", axis=0, tiled=True)

    run = functools.partial(
        two_sections,
        pos,
        band_rows,
        window_table,
        embed=embed_weight,
        level=level_embed,
        gains=gains,
        head=head_weight,
        own=own,
        other=other,
    )
    idle = jnp.zeros((1, WTOK, embed_weight.shape[1]), BF)
    h1, _, _ = run(own_raw[None], idle)
    c1 = swap(h1, "xh", 1)
    h2, _, _ = run(far_raw[None], h1)
    c2 = swap(h2, "xh", 1)
    _, out1, rows1 = run(far_raw[None], c1)
    back1, back_rows1 = swap(out1, "xh", 1), swap(rows1, "xh", 1)
    _, out2, rows2 = run(far_raw[None], c2)
    window_decoded = jnp.where(is_late, out2, back1)
    own_rows = jnp.where(is_late, rows2, back_rows1)

    reply = small_call(unpick_kernel, 2 * lat_count, scalars, to_rows(own_rows[0]), "unpick")
    came_back = lax.all_to_all(reply, LAT, 0, 0, tiled=True)
    decoded_rows = small_call(unpack_kernel, 2 * LW, scalars, came_back, "unpack")
    decoded = from_rows(decoded_rows)[None]
    return (decoded, window_decoded)


def solution(mesh):
    fine = Mesh(mesh.devices.reshape(2, 2, 8, 8, 2), ("xh", "c", "z", "y", "xl"))
    segment = ("xh", "c")
    placed = (
        P(segment, LAT, None),
        P(),
        P(),
        P(),
        P(),
        P(segment, None, LAT),
        P(segment, None),
        P(),
    )
    return jax.shard_map(
        per_device,
        mesh=fine,
        in_specs=placed,
        out_specs=(P(segment, LAT, None), P(segment, LAT, None)),
        check_vma=False,
    )
```

```python
import functools
import math

import jax
import jax.numpy as jnp
from jax import lax
from jax.experimental import pallas as pl
from jax.experimental.pallas import tpu as pltpu
from jax.sharding import Mesh
from jax.sharding import PartitionSpec as P

HEAD_DIM = 64
LEV = 2
WIN_ROWS = 12
WIN_COLS = 6
WTOK = 144
FEAT = 144
LW = 7
PIECE = WIN_COLS * LEV * FEAT
PACK = 16
BF = jnp.bfloat16
F32 = jnp.float32
LAT = ("z", "y", "xl")
DOUBLING = (4, 2, 1)
OFFS = (0, 4, 2, 6, 1, 5, 3, 7)
MIB = 1 << 20

VMEM = pl.BlockSpec(memory_space=pltpu.VMEM)
SMEM = pl.BlockSpec(memory_space=pltpu.SMEM)
ANY = pl.BlockSpec(memory_space=pl.ANY)


def ring(value, axis, by):
    n = lax.axis_size(axis)
    return lax.ppermute(value, axis, [(i, (i + by) % n) for i in range(n)])


def swap(value, axis, bit):
    n = lax.axis_size(axis)
    return lax.ppermute(value, axis, [(i, i ^ bit) for i in range(n)])


def pack_kernel(table, rows_ref, out_ref):
    @pl.loop(0, table.shape[0])
    def _(j):
        column = lax.rem(jnp.maximum(table[j], 0), LW)
        out_ref[2 * j] = rows_ref[column]
        out_ref[2 * j + 1] = rows_ref[LW + column]


def pick_kernel(where, bands, table, came_ref, out_ref):
    window = table[where[0]]
    first = WIN_ROWS * lax.div(jnp.maximum(window, 0), LW) - WIN_ROWS // 2
    out_ref[...] = jnp.zeros_like(out_ref)

    def band(i, start):
        row = start - first
        count = bands[i]

        @pl.when((window >= 0) & (row >= 0) & (row < WIN_ROWS))
        def _():
            out_ref[row] = came_ref[2 * i]

        @pl.when((window >= 0) & (count > 1) & (row >= -1) & (row < WIN_ROWS - 1))
        def _():
            out_ref[row + 1] = came_ref[2 * i + 1]

        return start + count

    lax.fori_loop(0, bands.shape[0], band, jnp.int32(0))


def unpick_kernel(where, bands, table, rows_ref, out_ref):
    window = table[where[0]]
    first = WIN_ROWS * lax.div(jnp.maximum(window, 0), LW) - WIN_ROWS // 2

    def band(i, start):
        row = start - first
        out_ref[2 * i] = rows_ref[jnp.clip(row, 0, WIN_ROWS - 1)]
        out_ref[2 * i + 1] = rows_ref[jnp.clip(row + 1, 0, WIN_ROWS - 1)]
        return start + bands[i]

    lax.fori_loop(0, bands.shape[0], band, jnp.int32(0))


def unpack_kernel(where, bands, table, came_ref, out_ref):
    mine = where[0]
    start = lax.fori_loop(0, mine, lambda i, total: total + bands[i], jnp.int32(0))
    count = bands[mine]
    wide = lax.div(start + WIN_ROWS // 2, WIN_ROWS)
    wide_next = lax.div(start + 1 + WIN_ROWS // 2, WIN_ROWS)
    out_ref[...] = jnp.zeros_like(out_ref)

    @pl.loop(0, table.shape[0])
    def _(j):
        window = table[j]
        across = lax.div(jnp.maximum(window, 0), LW)
        column = lax.rem(jnp.maximum(window, 0), LW)

        @pl.when((window >= 0) & (across == wide))
        def _():
            out_ref[column] = came_ref[2 * j]

        @pl.when((window >= 0) & (count > 1) & (across == wide_next))
        def _():
            out_ref[LW + column] = came_ref[2 * j + 1]


def to_rows(tokens):
    rows = tokens.reshape(-1, PIECE)
    return jnp.pad(rows, ((0, 0), (0, PACK * 128 - PIECE))).reshape(-1, PACK, 128)


def from_rows(rows):
    return rows.reshape(-1, PACK * 128)[:, :PIECE].reshape(-1, FEAT)


def join_kernel(pos, *refs):
    out_ref, out, sem = refs[-3:]
    pieces = refs[:-3]
    half = len(pieces) // 2
    z, y = pos[1], pos[2]

    def copies(side, index):
        ref = pieces[side * half + index]
        step = (0, -1, -2, -3, 1, 2, 3, 4, 4)[index]
        subs = range(8) if index < 7 else (range(4) if index == 7 else range(4, 8))
        for slot, sub in enumerate(subs):
            if side == 0:
                plane, line = lax.rem(z + step + 8, 8), y ^ OFFS[sub]
            else:
                plane, line = z ^ OFFS[sub], lax.rem(y + step + 8, 8)
            row = pl.multiple_of((plane * 8 + line) * 64, 64)
            yield pltpu.make_async_copy(
                ref.at[pl.ds(slot * 64, 64)], out.at[side, pl.ds(row, 64)], sem
            )

    every = [c for side in range(2) for i in range(half) for c in copies(side, i)]
    for c in every:
        c.start()
    for c in every:
        c.wait()
    back = pltpu.make_async_copy(out, out_ref, sem)
    back.start()
    back.wait()


def gather_section(weight, pos, message, arrived):
    mine, _ = lax.optimization_barrier((weight[0].T, message))
    pair = lax.all_gather(mine, "xl", axis=0, tiled=True)
    a, b = pair[:, :512], pair[:, 512:]
    for bit in DOUBLING:
        a_far, b_far = swap(a, "y", bit), swap(b, "z", bit)
        a, b = jnp.concatenate([a, a_far]), jnp.concatenate([b, b_far])
    pieces = []
    chains = [(a, "z", 1), (a, "z", -1), (b, "y", 1), (b, "y", -1)]
    got = [[] for _ in chains]
    held = [c[0] for c in chains]
    for step in range(4):
        if step == 3:
            *held, arrived = lax.optimization_barrier((*held, arrived))
        for n, (_, axis, by) in enumerate(chains):
            value = held[n]
            if step == 3:
                value = value[:256] if by > 0 else value[256:]
            held[n] = ring(value, axis, by)
            got[n].append(held[n])
    for own, ahead, behind in ((a, got[0], got[1]), (b, got[2], got[3])):
        pieces += [own, *ahead[:3], *behind[:3], ahead[3], behind[3]]
    return pl.pallas_call(
        join_kernel,
        out_shape=jax.ShapeDtypeStruct((2, 4096, 512), BF),
        in_specs=[SMEM] + [ANY] * len(pieces),
        out_specs=ANY,
        scratch_shapes=[pltpu.VMEM((2, 4096, 512), BF), pltpu.SemaphoreType.DMA(())],
        compiler_params=pltpu.CompilerParams(vmem_limit_bytes=60 * MIB),
        name="join",
    )(pos, *pieces), arrived


def matmul_t(left, right):
    return lax.dot_general(left, right, (((1,), (1,)), ((), ())), preferred_element_type=F32)


def block(hidden, gain, weights, wait, allowed):
    wide = hidden.astype(F32)
    scale = lax.rsqrt(jnp.mean(wide * wide, axis=-1, keepdims=True) + 1e-06)
    normed = (wide * scale * gain).astype(BF)

    def project(left, part):
        wait(part)
        rows = slice(1024 * part, 1024 * (part + 1))
        return matmul_t(left[:, :512], weights[0, rows]) + matmul_t(left[:, 512:], weights[1, rows])

    query = (project(normed, 0).astype(BF).astype(F32) * (1 / math.sqrt(HEAD_DIM))).astype(BF)
    keyed = project(normed, 1).astype(BF)
    valued = project(normed, 2).astype(BF)
    low = lax.broadcasted_iota(jnp.int32, (WTOK, 128), 1) < HEAD_DIM
    slabs = hidden.shape[0] // WTOK
    all_mixed = []
    for slab in range(slabs):
        here = slice(WTOK * slab, WTOK * (slab + 1))
        mixed = []
        for two in range(8):
            lanes = slice(128 * two, 128 * (two + 1))
            q2, k2, v2 = query[here, lanes], keyed[here, lanes], valued[here, lanes]
            outs = []
            for part in range(2):
                q1 = jnp.where(low if part == 0 else ~low, q2, jnp.zeros_like(q2))
                scores = jnp.where(allowed, matmul_t(q1, k2), -1e30)
                top = jnp.max(scores, axis=-1, keepdims=True)
                grown = jnp.exp(scores - top)
                probs = (grown / jnp.sum(grown, axis=-1, keepdims=True)).astype(BF)
                outs.append(jnp.dot(probs, v2, preferred_element_type=F32))
            mixed.append(jnp.where(low, outs[0], outs[1]).astype(BF))
        all_mixed.append(jnp.concatenate(mixed, axis=1))
    mixed = jnp.concatenate(all_mixed, axis=0) if slabs > 1 else all_mixed[0]
    return (wide + project(mixed, 3)).astype(BF)


def sections_kernel(
    pos, bands, table, raw_ref, came_ref, embed_ref, level_ref, gain_ref, head_ref, own_ref, other_ref,
    hidden_ref, out_ref, rows_ref, weights, sems,
):
    core, late = pos[3], pos[4]

    def load(source, section):
        for part in range(4):
            rows = pl.ds(1024 * part, 1024)
            pltpu.make_async_copy(
                source.at[:, rows], weights.at[section, :, rows], sems.at[section, part]
            ).start()

    @pl.when(core == 0)
    def _():
        load(own_ref, 0)
        load(other_ref, 1)

    @pl.when(core == 1)
    def _():
        load(other_ref, 0)
        load(own_ref, 1)

    def waiter(section):
        def wait(part):
            rows = pl.ds(1024 * part, 1024)
            pltpu.make_async_copy(
                own_ref.at[:, rows], weights.at[section, :, rows], sems.at[section, part]
            ).wait()

        return wait

    slabs = raw_ref.shape[0]
    query_token = lax.broadcasted_iota(jnp.int32, (WTOK, WTOK), 0)
    key_token = lax.broadcasted_iota(jnp.int32, (WTOK, WTOK), 1)
    half = WIN_ROWS * WIN_COLS
    same = lax.rem(query_token, half) == lax.rem(key_token, half)
    window = table[pos[0]]
    first = WIN_ROWS * lax.div(jnp.maximum(window, 0), LW) - WIN_ROWS // 2
    total_rows = 3 * bands.shape[0] // 2

    def inside(token):
        row = first + lax.rem(lax.div(token, WIN_COLS), WIN_ROWS)
        return (window >= 0) & (row >= 0) & (row < total_rows)

    keep = inside(key_token)
    is_late = late == 1
    first_mask = (same & (late == 0)) | (keep & (late == 1))
    second_mask = (keep & (late == 0)) | (same & (late == 1))
    to_window = (lax.div(query_token, half) == lax.rem(key_token, LEV)) & (
        lax.rem(query_token, half) == lax.div(key_token, LEV)
    )
    from_window = (lax.rem(query_token, LEV) == lax.div(key_token, half)) & (
        lax.div(query_token, LEV) == lax.rem(key_token, half)
    )
    to_window = to_window.astype(BF)
    from_window = from_window.astype(BF)
    upper = lax.broadcasted_iota(jnp.int32, (WTOK, 1), 0) < half
    level_rows = jnp.where(upper, level_ref[0:1].astype(F32), level_ref[1:2].astype(F32))
    starts = []
    for slab in range(slabs):
        raw = jnp.dot(to_window, raw_ref[slab], preferred_element_type=F32).astype(BF)
        embedded = (jnp.dot(raw, embed_ref[...], preferred_element_type=F32) + level_rows).astype(BF)
        starts.append(jnp.where(is_late, came_ref[slab], embedded))
    hidden = jnp.concatenate(starts, axis=0) if slabs > 1 else starts[0]
    hidden = block(hidden, gain_ref[0:1], weights.at[0], waiter(0), first_mask)
    hidden = block(hidden, gain_ref[1:2], weights.at[1], waiter(1), second_mask)
    result = jnp.dot(hidden, head_ref[...], preferred_element_type=F32)
    keep_row = inside(lax.broadcasted_iota(jnp.int32, (WTOK, 1), 0))
    for slab in range(slabs):
        here = slice(WTOK * slab, WTOK * (slab + 1))
        hidden_ref[slab] = hidden[here]
        out = jnp.where(keep_row, result[here], 0.0).astype(BF)
        out_ref[slab] = out
        rows_ref[slab] = jnp.dot(from_window, out, preferred_element_type=F32).astype(BF)


def two_sections(pos, bands, table, raw, came, embed, level, gains, head, own, other):
    slabs = raw.shape[0]
    width = embed.shape[1]
    return pl.pallas_call(
        sections_kernel,
        out_shape=(
            jax.ShapeDtypeStruct((slabs, WTOK, width), BF),
            jax.ShapeDtypeStruct((slabs, WTOK, FEAT), BF),
            jax.ShapeDtypeStruct((slabs, WTOK, FEAT), BF),
        ),
        in_specs=[SMEM] * 3 + [VMEM] * 6 + [ANY] * 2,
        out_specs=(VMEM,) * 3,
        scratch_shapes=[
            pltpu.VMEM((2, 2, 4096, 512), BF),
            pltpu.SemaphoreType.DMA((2, 4)),
        ],
        compiler_params=pltpu.CompilerParams(vmem_limit_bytes=30 * MIB),
        name="sections",
    )(pos, bands, table, raw, came, embed, level, gains, head, own, other)


def small_call(body, out_rows, scalars, value, name):
    return pl.pallas_call(
        body,
        out_shape=jax.ShapeDtypeStruct((out_rows, PACK, 128), BF),
        in_specs=[SMEM] * len(scalars) + [VMEM],
        out_specs=VMEM,
        name=name,
    )(*scalars, value)


def per_device(
    fields, band_rows, window_table, level_embed, embed_weight, attn_weight, norm_gain, head_weight
):
    late, core = lax.axis_index("xh"), lax.axis_index("c")
    pos = jnp.stack([lax.axis_index(LAT), lax.axis_index("z"), lax.axis_index("y"), core, late])
    scalars = (pos, band_rows, window_table)
    lat_count = band_rows.shape[0]
    is_late = late == 1

    message = small_call(pack_kernel, 2 * lat_count, (window_table,), to_rows(fields[0]), "pack")
    arrived = lax.all_to_all(message, LAT, 0, 0, tiled=True)
    own, arrived = gather_section(attn_weight, pos, message, arrived)
    raw_rows = small_call(pick_kernel, WIN_ROWS, scalars, arrived, "pick")
    own_raw = from_rows(raw_rows)
    far_raw = swap(own_raw, "xh", 1)

    other = swap(own, "c", 1)
    gains = lax.all_gather(norm_gain, "c", axis=0, tiled=True)

    run = functools.partial(
        two_sections,
        pos,
        band_rows,
        window_table,
        embed=embed_weight,
        level=level_embed,
        gains=gains,
        head=head_weight,
        own=own,
        other=other,
    )
    idle = jnp.zeros((1, WTOK, embed_weight.shape[1]), BF)
    h1, _, _ = run(own_raw[None], idle)
    c1 = swap(h1, "xh", 1)
    h2, _, _ = run(far_raw[None], h1)
    c2 = swap(h2, "xh", 1)
    _, out1, rows1 = run(far_raw[None], c1)
    back1, back_rows1 = swap(out1, "xh", 1), swap(rows1, "xh", 1)
    _, out2, rows2 = run(far_raw[None], c2)
    window_decoded = jnp.where(is_late, out2, back1)
    own_rows = jnp.where(is_late, rows2, back_rows1)

    reply = small_call(unpick_kernel, 2 * lat_count, scalars, to_rows(own_rows[0]), "unpick")
    came_back = lax.all_to_all(reply, LAT, 0, 0, tiled=True)
    decoded_rows = small_call(unpack_kernel, 2 * LW, scalars, came_back, "unpack")
    decoded = from_rows(decoded_rows)[None]
    return (decoded, window_decoded)


def solution(mesh):
    fine = Mesh(mesh.devices.reshape(2, 2, 8, 8, 2), ("xh", "c", "z", "y", "xl"))
    segment = ("xh", "c")
    placed = (
        P(segment, LAT, None),
        P(),
        P(),
        P(),
        P(),
        P(segment, None, LAT),
        P(segment, None),
        P(),
    )
    return jax.shard_map(
        per_device,
        mesh=fine,
        in_specs=placed,
        out_specs=(P(segment, LAT, None), P(segment, LAT, None)),
        check_vma=False,
    )
```

```python
import functools
import math

import jax
import jax.numpy as jnp
from jax import lax
from jax.experimental import pallas as pl
from jax.experimental.pallas import tpu as pltpu
from jax.sharding import Mesh
from jax.sharding import PartitionSpec as P

HEAD_DIM = 64
LEV = 2
WIN_ROWS = 12
WIN_COLS = 6
WTOK = 144
FEAT = 144
LW = 7
PIECE = WIN_COLS * LEV * FEAT
PACK = 16
BF = jnp.bfloat16
F32 = jnp.float32
LAT = ("z", "y", "xl")
DOUBLING = (4, 2, 1)
OFFS = (0, 4, 2, 6, 1, 5, 3, 7)
MIB = 1 << 20

VMEM = pl.BlockSpec(memory_space=pltpu.VMEM)
SMEM = pl.BlockSpec(memory_space=pltpu.SMEM)
ANY = pl.BlockSpec(memory_space=pl.ANY)


def ring(value, axis, by):
    n = lax.axis_size(axis)
    return lax.ppermute(value, axis, [(i, (i + by) % n) for i in range(n)])


def swap(value, axis, bit):
    n = lax.axis_size(axis)
    return lax.ppermute(value, axis, [(i, i ^ bit) for i in range(n)])


def seventh(window):
    return lax.shift_right_logical(window * 147, 10)


def first_row(window):
    return WIN_ROWS * seventh(jnp.maximum(window, 0)) - WIN_ROWS // 2


def pack_kernel(table, rows_ref, out_ref):
    def shard(j, carry):
        window = jnp.maximum(table[j], 0)
        column = window - LW * seventh(window)
        out_ref[2 * j] = rows_ref[column]
        out_ref[2 * j + 1] = rows_ref[LW + column]
        return carry

    lax.fori_loop(0, table.shape[0], shard, 0, unroll=8)


def pick_kernel(where, bands, table, came_ref, out_ref):
    window = table[where[0]]
    first = first_row(window)
    out_ref[...] = jnp.zeros_like(out_ref)
    count_rows = jnp.where(window >= 0, WIN_ROWS, 0)

    def band(i, row):
        count = bands[i]
        here = (row >= 0) & (row < count_rows)
        out_ref[jnp.where(here, row, WIN_ROWS)] = came_ref[2 * i]
        here = (count > 1) & (row >= -1) & (row + 1 < count_rows)
        out_ref[jnp.where(here, row + 1, WIN_ROWS)] = came_ref[2 * i + 1]
        return row + count

    lax.fori_loop(0, bands.shape[0], band, -first, unroll=8)


def unpick_kernel(where, bands, table, rows_ref, out_ref):
    first = first_row(table[where[0]])

    def band(i, row):
        out_ref[2 * i] = rows_ref[jnp.clip(row, 0, WIN_ROWS - 1)]
        out_ref[2 * i + 1] = rows_ref[jnp.clip(row + 1, 0, WIN_ROWS - 1)]
        return row + bands[i]

    lax.fori_loop(0, bands.shape[0], band, -first, unroll=8)


def unpack_kernel(where, bands, table, came_ref, out_ref):
    mine = where[0]
    start = lax.fori_loop(
        0, bands.shape[0], lambda i, total: total + jnp.where(i < mine, bands[i], 0), jnp.int32(0), unroll=8
    )
    across = lax.div(start + WIN_ROWS // 2, WIN_ROWS)
    across_next = jnp.where(bands[mine] > 1, lax.div(start + 1 + WIN_ROWS // 2, WIN_ROWS), -1)
    out_ref[...] = jnp.zeros_like(out_ref)

    def shard(j, carry):
        window = jnp.maximum(table[j], 0)
        line = jnp.where(table[j] >= 0, seventh(window), -2)
        column = window - LW * seventh(window)
        out_ref[jnp.where(line == across, column, 2 * LW)] = came_ref[2 * j]
        out_ref[jnp.where(line == across_next, LW + column, 2 * LW)] = came_ref[2 * j + 1]
        return carry

    lax.fori_loop(0, table.shape[0], shard, 0, unroll=8)


def to_rows(tokens):
    rows = tokens.reshape(-1, PIECE)
    return jnp.pad(rows, ((0, 0), (0, PACK * 128 - PIECE))).reshape(-1, PACK, 128)


def from_rows(rows):
    return rows.reshape(-1, PACK * 128)[:, :PIECE].reshape(-1, FEAT)


def join_kernel(pos, *refs):
    out_ref, out, turned, sem = refs[-4:]
    pieces = refs[:-4]
    half = len(pieces) // 2
    z, y = pos[1], pos[2]

    def copies(side, index):
        ref = pieces[side * half + index]
        step = (0, -1, -2, -3, 1, 2, 3, 4)[index]
        for slot, sub in enumerate(range(8)):
            if side == 0:
                plane, line = lax.rem(z + step + 8, 8), y ^ OFFS[sub]
            else:
                plane, line = z ^ OFFS[sub], lax.rem(y + step + 8, 8)
            row = pl.multiple_of((plane * 8 + line) * 64, 64)
            yield pltpu.make_async_copy(
                ref.at[pl.ds(slot * 64, 64)], out.at[side, pl.ds(row, 64)], sem
            )

    every = [c for side in range(2) for i in range(half) for c in copies(side, i)]
    for c in every:
        c.start()
    for c in every:
        c.wait()

    @pl.loop(0, 8)
    def _(plane):
        lanes = pl.ds(pl.multiple_of(plane * 512, 512), 512)
        for side in range(2):
            turned[512 * side : 512 * (side + 1), lanes] = out[side, lanes, :].T

    back = pltpu.make_async_copy(turned, out_ref, sem)
    back.start()
    back.wait()


def gather_section(weight, pos, message, arrived, gains):
    mine, _ = lax.optimization_barrier((weight[0].T, message))
    pair = lax.all_gather(mine, "xl", axis=0, tiled=True)
    pair, gains = lax.optimization_barrier((pair, gains))
    a, b = pair[:, :512], pair[:, 512:]
    for bit in DOUBLING:
        a_far, b_far = swap(a, "y", bit), swap(b, "z", bit)
        a, b = jnp.concatenate([a, a_far]), jnp.concatenate([b, b_far])
    a, b, arrived = lax.optimization_barrier((a, b, arrived))
    chains = [("z", 1), ("z", -1), ("y", 1), ("y", -1)]
    got = [[] for _ in chains]
    held = [a, a, b, b]
    for step in range(4):
        for n, (axis, by) in enumerate(chains):
            if step < 3 or by > 0:
                held[n] = ring(held[n], axis, by)
                got[n].append(held[n])
    pieces = []
    for own, ahead, behind in ((a, got[0], got[1]), (b, got[2], got[3])):
        pieces += [own, *ahead[:3], *behind, ahead[3]]
    section = pl.pallas_call(
        join_kernel,
        out_shape=jax.ShapeDtypeStruct((1024, 4096), BF),
        in_specs=[SMEM] + [ANY] * len(pieces),
        out_specs=ANY,
        scratch_shapes=[
            pltpu.VMEM((2, 4096, 512), BF),
            pltpu.VMEM((1024, 4096), BF),
            pltpu.SemaphoreType.DMA(()),
        ],
        compiler_params=pltpu.CompilerParams(vmem_limit_bytes=60 * MIB),
        name="join",
    )(pos, *pieces)
    return section, arrived, gains


def matmul_t(left, right):
    return lax.dot_general(left, right, (((1,), (1,)), ((), ())), preferred_element_type=F32)


def normed_of(wide, gain):
    scale = lax.rsqrt(jnp.mean(wide * wide, axis=-1, keepdims=True) + 1e-06)
    return (wide * scale * gain).astype(BF)


def project(left, weights, wait, part):
    wait(part)
    return jnp.dot(left, weights[:, 1024 * part : 1024 * (part + 1)], preferred_element_type=F32)


def column_block(hidden, gain, weights, wait):
    wide = hidden.astype(F32)
    normed = normed_of(wide, gain)
    half = WTOK // 2

    def other_level(value):
        return jnp.concatenate([value[half:], value[:half]], axis=0)

    query = project(normed, weights, wait, 0).astype(BF).astype(F32)
    keyed = project(normed, weights, wait, 1).astype(BF).astype(F32)
    product = query * (keyed - other_level(keyed))
    lane = lax.broadcasted_iota(jnp.int32, (1024, 128), 0)
    head = lax.broadcasted_iota(jnp.int32, (1024, 128), 1)
    of_head = (lax.div(lane, HEAD_DIM) == head).astype(BF)
    high = product.astype(BF)
    low = (product - high.astype(F32)).astype(BF)
    gap = (
        jnp.dot(high, of_head, preferred_element_type=F32)
        + jnp.dot(low, of_head, preferred_element_type=F32)
    ) * (1 / math.sqrt(HEAD_DIM))
    small = jnp.exp(-jnp.abs(gap))
    larger = 1.0 / (1.0 + small)
    smaller = small * larger
    own = jnp.where(gap >= 0, larger, smaller).astype(BF)
    far = jnp.where(gap >= 0, smaller, larger).astype(BF)
    valued = project(normed, weights, wait, 2).astype(BF).astype(F32)
    mixed = (matmul_t(own, of_head) * valued + matmul_t(far, of_head) * other_level(valued)).astype(BF)
    return (wide + project(mixed, weights, wait, 3)).astype(BF)


def window_block(hidden, gain, weights, wait, bias):
    wide = hidden.astype(F32)
    normed = normed_of(wide, gain)
    query = (project(normed, weights, wait, 0).astype(BF).astype(F32) * (1 / math.sqrt(HEAD_DIM))).astype(BF)
    keyed = project(normed, weights, wait, 1).astype(BF)
    valued = project(normed, weights, wait, 2).astype(BF)
    low = lax.broadcasted_iota(jnp.int32, (WTOK, 128), 1) < HEAD_DIM
    ones = jnp.ones((WTOK, 128), BF)
    mixed = []
    for two in range(8):
        lanes = slice(128 * two, 128 * (two + 1))
        q2, k2 = query[:, lanes], keyed[:, lanes]
        v2 = jnp.concatenate([valued[:, lanes], ones], axis=1)
        outs = []
        for part in range(2):
            q1 = jnp.where(low if part == 0 else ~low, q2, jnp.zeros_like(q2))
            scores = matmul_t(q1, k2) + bias
            top = jnp.max(scores, axis=-1, keepdims=True)
            grown = jnp.exp(scores - top).astype(BF)
            summed = jnp.dot(grown, v2, preferred_element_type=F32)
            outs.append(summed[:, :128] / summed[:, 128:])
        mixed.append(jnp.where(low, outs[0], outs[1]).astype(BF))
    mixed = jnp.concatenate(mixed, axis=1)
    return (wide + project(mixed, weights, wait, 3)).astype(BF)


def sections_kernel(
    pos, bands, table, raw_ref, came_ref, embed_ref, level_ref, gain_ref, head_ref, own_ref, other_ref,
    hidden_ref, out_ref, rows_ref, weights, sems,
):
    core, late = pos[3], pos[4]

    def load(source, section):
        for part in range(4):
            columns = pl.ds(1024 * part, 1024)
            pltpu.make_async_copy(
                source.at[:, columns], weights.at[section, :, columns], sems.at[section, part]
            ).start()

    @pl.when(core == 0)
    def _():
        load(own_ref, 0)
        load(other_ref, 1)

    @pl.when(core == 1)
    def _():
        load(other_ref, 0)
        load(own_ref, 1)

    def waiter(section):
        def wait(part):
            columns = pl.ds(1024 * part, 1024)
            pltpu.make_async_copy(
                own_ref.at[:, columns], weights.at[section, :, columns], sems.at[section, part]
            ).wait()

        return wait

    query_token = lax.broadcasted_iota(jnp.int32, (WTOK, WTOK), 0)
    key_token = lax.broadcasted_iota(jnp.int32, (WTOK, WTOK), 1)
    half = WIN_ROWS * WIN_COLS
    window = table[pos[0]]
    first = first_row(window)
    total_rows = 3 * bands.shape[0] // 2

    def inside(token):
        row = first + lax.rem(lax.div(token, WIN_COLS), WIN_ROWS)
        return (window >= 0) & (row >= 0) & (row < total_rows)

    bias = jnp.where(inside(lax.broadcasted_iota(jnp.int32, (1, WTOK), 1)), 0.0, -1e30)

    @pl.when(late == 0)
    def _():
        to_window = (lax.div(query_token, half) == lax.rem(key_token, LEV)) & (
            lax.rem(query_token, half) == lax.div(key_token, LEV)
        )
        upper = lax.broadcasted_iota(jnp.int32, (WTOK, 1), 0) < half
        level_rows = jnp.where(upper, level_ref[0:1].astype(F32), level_ref[1:2].astype(F32))
        raw = jnp.dot(to_window.astype(BF), raw_ref[0], preferred_element_type=F32).astype(BF)
        hidden = (jnp.dot(raw, embed_ref[...], preferred_element_type=F32) + level_rows).astype(BF)
        hidden = column_block(hidden, gain_ref[0:1], weights.at[0], waiter(0))
        hidden_ref[0] = window_block(hidden, gain_ref[1:2], weights.at[1], waiter(1), bias)
        out_ref[...] = jnp.zeros_like(out_ref)
        rows_ref[...] = jnp.zeros_like(rows_ref)

    @pl.when(late == 1)
    def _():
        hidden = window_block(came_ref[0], gain_ref[0:1], weights.at[0], waiter(0), bias)
        hidden = column_block(hidden, gain_ref[1:2], weights.at[1], waiter(1))
        hidden_ref[0] = hidden
        result = jnp.dot(hidden, head_ref[...], preferred_element_type=F32)
        keep_row = inside(lax.broadcasted_iota(jnp.int32, (WTOK, 1), 0))
        out = jnp.where(keep_row, result, 0.0).astype(BF)
        out_ref[0] = out
        from_window = (lax.rem(query_token, LEV) == lax.div(key_token, half)) & (
            lax.div(query_token, LEV) == lax.rem(key_token, half)
        )
        rows_ref[0] = jnp.dot(from_window.astype(BF), out, preferred_element_type=F32).astype(BF)


def two_sections(pos, bands, table, raw, came, embed, level, gains, head, own, other):
    slabs = raw.shape[0]
    width = embed.shape[1]
    return pl.pallas_call(
        sections_kernel,
        out_shape=(
            jax.ShapeDtypeStruct((slabs, WTOK, width), BF),
            jax.ShapeDtypeStruct((slabs, WTOK, FEAT), BF),
            jax.ShapeDtypeStruct((slabs, WTOK, FEAT), BF),
        ),
        in_specs=[SMEM] * 3 + [VMEM] * 6 + [ANY] * 2,
        out_specs=(VMEM,) * 3,
        scratch_shapes=[
            pltpu.VMEM((2, 1024, 4096), BF),
            pltpu.SemaphoreType.DMA((2, 4)),
        ],
        compiler_params=pltpu.CompilerParams(vmem_limit_bytes=60 * MIB),
        name="sections",
    )(pos, bands, table, raw, came, embed, level, gains, head, own, other)


def small_call(body, out_rows, scalars, value, name):
    return pl.pallas_call(
        body,
        out_shape=jax.ShapeDtypeStruct((out_rows, PACK, 128), BF),
        in_specs=[SMEM] * len(scalars) + [VMEM],
        out_specs=VMEM,
        name=name,
    )(*scalars, value)


def per_device(
    fields, band_rows, window_table, level_embed, embed_weight, attn_weight, norm_gain, head_weight
):
    late, core = lax.axis_index("xh"), lax.axis_index("c")
    pos = jnp.stack([lax.axis_index(LAT), lax.axis_index("z"), lax.axis_index("y"), core, late])
    scalars = (pos, band_rows, window_table)
    lat_count = band_rows.shape[0]
    is_late = late == 1

    message = small_call(pack_kernel, 2 * lat_count, (window_table,), to_rows(fields[0]), "pack")
    arrived = lax.all_to_all(message, LAT, 0, 0, tiled=True)
    gains = lax.all_gather(norm_gain, "c", axis=0, tiled=True)
    own, arrived, gains = gather_section(attn_weight, pos, message, arrived, gains)
    raw_rows = small_call(pick_kernel, WIN_ROWS + 1, scalars, arrived, "pick")
    own_raw = from_rows(raw_rows[:WIN_ROWS])
    far_raw = swap(own_raw, "xh", 1)

    other = swap(own, "c", 1)

    run = functools.partial(
        two_sections,
        pos,
        band_rows,
        window_table,
        embed=embed_weight,
        level=level_embed,
        gains=gains,
        head=head_weight,
        own=own,
        other=other,
    )
    idle = jnp.zeros((1, WTOK, embed_weight.shape[1]), BF)
    h1, _, _ = run(own_raw[None], idle)
    c1 = swap(h1, "xh", 1)
    h2, _, _ = run(far_raw[None], h1)
    c2 = swap(h2, "xh", 1)
    _, out1, rows1 = run(far_raw[None], c1)
    back1, back_rows1 = swap(out1, "xh", 1), swap(rows1, "xh", 1)
    _, out2, rows2 = run(far_raw[None], c2)
    window_decoded = jnp.where(is_late, out2, back1)
    own_rows = jnp.where(is_late, rows2, back_rows1)

    reply = small_call(unpick_kernel, 2 * lat_count, scalars, to_rows(own_rows[0]), "unpick")
    came_back = lax.all_to_all(reply, LAT, 0, 0, tiled=True)
    decoded_rows = small_call(unpack_kernel, 2 * LW + 1, scalars, came_back, "unpack")
    decoded = from_rows(decoded_rows[: 2 * LW])[None]
    return (decoded, window_decoded)


def solution(mesh):
    fine = Mesh(mesh.devices.reshape(2, 2, 8, 8, 2), ("xh", "c", "z", "y", "xl"))
    segment = ("xh", "c")
    placed = (
        P(segment, LAT, None),
        P(),
        P(),
        P(),
        P(),
        P(segment, None, LAT),
        P(segment, None),
        P(),
    )
    return jax.shard_map(
        per_device,
        mesh=fine,
        in_specs=placed,
        out_specs=(P(segment, LAT, None), P(segment, LAT, None)),
        check_vma=False,
    )
```

```python
import math

import jax
import jax.numpy as jnp
from jax import lax
from jax.experimental import pallas as pl
from jax.experimental.pallas import tpu as pltpu
from jax.sharding import Mesh
from jax.sharding import PartitionSpec as P

HEAD_DIM = 64
LEV = 2
WIN_ROWS = 12
WIN_COLS = 6
WTOK = 144
FEAT = 144
LW = 7
PIECE = WIN_COLS * LEV * FEAT
PACK = 16
BF = jnp.bfloat16
F32 = jnp.float32
LAT = ("z", "y", "xl")
DOUBLING = (4, 2, 1)
OFFS = (0, 4, 2, 6, 1, 5, 3, 7)
MIB = 1 << 20

VMEM = pl.BlockSpec(memory_space=pltpu.VMEM)
SMEM = pl.BlockSpec(memory_space=pltpu.SMEM)
ANY = pl.BlockSpec(memory_space=pl.ANY)


def ring(value, axis, by):
    n = lax.axis_size(axis)
    return lax.ppermute(value, axis, [(i, (i + by) % n) for i in range(n)])


def swap(value, axis, bit):
    n = lax.axis_size(axis)
    return lax.ppermute(value, axis, [(i, i ^ bit) for i in range(n)])


def seventh(window):
    return lax.shift_right_logical(window * 147, 10)


def first_row(window):
    return WIN_ROWS * seventh(jnp.maximum(window, 0)) - WIN_ROWS // 2


def pack_kernel(table, rows_ref, out_ref):
    def shard(j, carry):
        window = jnp.maximum(table[j], 0)
        column = window - LW * seventh(window)
        out_ref[2 * j] = rows_ref[column]
        out_ref[2 * j + 1] = rows_ref[LW + column]
        return carry

    lax.fori_loop(0, table.shape[0], shard, 0, unroll=8)


def pick_kernel(where, bands, table, came_ref, out_ref):
    window = table[where[0]]
    first = first_row(window)
    out_ref[...] = jnp.zeros_like(out_ref)
    count_rows = jnp.where(window >= 0, WIN_ROWS, 0)

    def band(i, row):
        count = bands[i]
        here = (row >= 0) & (row < count_rows)
        out_ref[jnp.where(here, row, WIN_ROWS)] = came_ref[2 * i]
        here = (count > 1) & (row >= -1) & (row + 1 < count_rows)
        out_ref[jnp.where(here, row + 1, WIN_ROWS)] = came_ref[2 * i + 1]
        return row + count

    lax.fori_loop(0, bands.shape[0], band, -first, unroll=8)


def unpick_kernel(where, bands, table, rows_ref, out_ref):
    first = first_row(table[where[0]])

    def band(i, row):
        out_ref[2 * i] = rows_ref[jnp.clip(row, 0, WIN_ROWS - 1)]
        out_ref[2 * i + 1] = rows_ref[jnp.clip(row + 1, 0, WIN_ROWS - 1)]
        return row + bands[i]

    lax.fori_loop(0, bands.shape[0], band, -first, unroll=8)


def unpack_kernel(where, bands, table, came_ref, out_ref):
    mine = where[0]
    start = lax.fori_loop(
        0, bands.shape[0], lambda i, total: total + jnp.where(i < mine, bands[i], 0), jnp.int32(0), unroll=8
    )
    across = lax.div(start + WIN_ROWS // 2, WIN_ROWS)
    across_next = jnp.where(bands[mine] > 1, lax.div(start + 1 + WIN_ROWS // 2, WIN_ROWS), -1)
    out_ref[...] = jnp.zeros_like(out_ref)

    def shard(j, carry):
        window = jnp.maximum(table[j], 0)
        line = jnp.where(table[j] >= 0, seventh(window), -2)
        column = window - LW * seventh(window)
        out_ref[jnp.where(line == across, column, 2 * LW)] = came_ref[2 * j]
        out_ref[jnp.where(line == across_next, LW + column, 2 * LW)] = came_ref[2 * j + 1]
        return carry

    lax.fori_loop(0, table.shape[0], shard, 0, unroll=8)


def to_rows(tokens):
    rows = tokens.reshape(-1, PIECE)
    return jnp.pad(rows, ((0, 0), (0, PACK * 128 - PIECE))).reshape(-1, PACK, 128)


def from_rows(rows):
    return rows.reshape(-1, PACK * 128)[:, :PIECE].reshape(-1, FEAT)


def join_kernel(pos, *refs):
    out_ref, out, turned, sem = refs[-4:]
    pieces = refs[:-4]
    half = len(pieces) // 2
    z, y = pos[1], pos[2]

    def copies(side, index):
        ref = pieces[side * half + index]
        step = (0, -1, -2, -3, 1, 2, 3, 4)[index]
        for slot, sub in enumerate(range(8)):
            if side == 0:
                plane, line = lax.rem(z + step + 8, 8), y ^ OFFS[sub]
            else:
                plane, line = z ^ OFFS[sub], lax.rem(y + step + 8, 8)
            row = pl.multiple_of((plane * 8 + line) * 64, 64)
            yield pltpu.make_async_copy(
                ref.at[pl.ds(slot * 64, 64)], out.at[side, pl.ds(row, 64)], sem
            )

    every = [c for side in range(2) for i in range(half) for c in copies(side, i)]
    for c in every:
        c.start()
    for c in every:
        c.wait()

    @pl.loop(0, 8)
    def _(plane):
        lanes = pl.ds(pl.multiple_of(plane * 512, 512), 512)
        for side in range(2):
            turned[512 * side : 512 * (side + 1), lanes] = out[side, lanes, :].T

    back = pltpu.make_async_copy(turned, out_ref, sem)
    back.start()
    back.wait()


def gather_section(weight, pos, message, arrived, gains):
    mine, _ = lax.optimization_barrier((weight[0].T, message))
    pair = lax.all_gather(mine, "xl", axis=0, tiled=True)
    pair, gains = lax.optimization_barrier((pair, gains))
    a, b = pair[:, :512], pair[:, 512:]
    for bit in DOUBLING:
        a_far, b_far = swap(a, "y", bit), swap(b, "z", bit)
        a, b = jnp.concatenate([a, a_far]), jnp.concatenate([b, b_far])
    a, b, arrived = lax.optimization_barrier((a, b, arrived))
    chains = [("z", 1), ("z", -1), ("y", 1), ("y", -1)]
    got = [[] for _ in chains]
    held = [a, a, b, b]
    for step in range(4):
        for n, (axis, by) in enumerate(chains):
            if step < 3 or by > 0:
                held[n] = ring(held[n], axis, by)
                got[n].append(held[n])
    pieces = []
    for own, ahead, behind in ((a, got[0], got[1]), (b, got[2], got[3])):
        pieces += [own, *ahead[:3], *behind, ahead[3]]
    section = pl.pallas_call(
        join_kernel,
        out_shape=jax.ShapeDtypeStruct((1024, 4096), BF),
        in_specs=[SMEM] + [ANY] * len(pieces),
        out_specs=ANY,
        scratch_shapes=[
            pltpu.VMEM((2, 4096, 512), BF),
            pltpu.VMEM((1024, 4096), BF),
            pltpu.SemaphoreType.DMA(()),
        ],
        compiler_params=pltpu.CompilerParams(vmem_limit_bytes=60 * MIB),
        name="join",
    )(pos, *pieces)
    return section, arrived, gains


def matmul_t(left, right):
    return lax.dot_general(left, right, (((1,), (1,)), ((), ())), preferred_element_type=F32)


def normed_of(wide, gain):
    scale = lax.rsqrt(jnp.mean(wide * wide, axis=-1, keepdims=True) + 1e-06)
    return (wide * scale * gain).astype(BF)


def other_level(value):
    half = WTOK // 2
    parts = [value[half * i : half * (i + 1)] for i in range(value.shape[0] // half)]
    return jnp.concatenate([parts[i ^ 1] for i in range(len(parts))], axis=0)


def column_block(hidden, gain, project):
    wide = hidden.astype(F32)
    normed = normed_of(wide, gain)
    query = project(normed, 0).astype(BF).astype(F32)
    keyed = project(normed, 1).astype(BF).astype(F32)
    product = query * (keyed - other_level(keyed))
    lane = lax.broadcasted_iota(jnp.int32, (1024, 128), 0)
    head = lax.broadcasted_iota(jnp.int32, (1024, 128), 1)
    of_head = (lax.div(lane, HEAD_DIM) == head).astype(BF)
    high = product.astype(BF)
    low = (product - high.astype(F32)).astype(BF)
    gap = (
        jnp.dot(high, of_head, preferred_element_type=F32)
        + jnp.dot(low, of_head, preferred_element_type=F32)
    ) * (1 / math.sqrt(HEAD_DIM))
    small = jnp.exp(-jnp.abs(gap))
    larger = 1.0 / (1.0 + small)
    smaller = small * larger
    own = jnp.where(gap >= 0, larger, smaller).astype(BF)
    far = jnp.where(gap >= 0, smaller, larger).astype(BF)
    valued = project(normed, 2).astype(BF).astype(F32)
    mixed = (matmul_t(own, of_head) * valued + matmul_t(far, of_head) * other_level(valued)).astype(BF)
    return (wide + project(mixed, 3)).astype(BF)


def window_block(hidden, gain, project, bias):
    wide = hidden.astype(F32)
    normed = normed_of(wide, gain)
    query = (project(normed, 0).astype(BF).astype(F32) * (1 / math.sqrt(HEAD_DIM))).astype(BF)
    keyed = project(normed, 1).astype(BF)
    valued = project(normed, 2).astype(BF)
    low = lax.broadcasted_iota(jnp.int32, (WTOK, 128), 1) < HEAD_DIM
    ones = jnp.ones((WTOK, 128), BF)
    slabs = []
    for slab in range(hidden.shape[0] // WTOK):
        here = slice(WTOK * slab, WTOK * (slab + 1))
        mixed = []
        for two in range(8):
            lanes = slice(128 * two, 128 * (two + 1))
            q2, k2 = query[here, lanes], keyed[here, lanes]
            v2 = jnp.concatenate([valued[here, lanes], ones], axis=1)
            outs = []
            for part in range(2):
                q1 = jnp.where(low if part == 0 else ~low, q2, jnp.zeros_like(q2))
                scores = matmul_t(q1, k2) + bias
                top = jnp.max(scores, axis=-1, keepdims=True)
                grown = jnp.exp(scores - top).astype(BF)
                summed = jnp.dot(grown, v2, preferred_element_type=F32)
                outs.append(summed[:, :128] / summed[:, 128:])
            mixed.append(jnp.where(low, outs[0], outs[1]).astype(BF))
        slabs.append(jnp.concatenate(mixed, axis=1))
    mixed = jnp.concatenate(slabs, axis=0)
    return (wide + project(mixed, 3)).astype(BF)


def projections(pos, own_ref, other_ref, weights, sems):
    core = pos[3]

    def load(source, section):
        for part in range(4):
            columns = pl.ds(1024 * part, 1024)
            pltpu.make_async_copy(
                source.at[:, columns], weights.at[section, :, columns], sems.at[section, part]
            ).start()

    @pl.when(core == 0)
    def _():
        load(own_ref, 0)
        load(other_ref, 1)

    @pl.when(core == 1)
    def _():
        load(other_ref, 0)
        load(own_ref, 1)

    def of_section(section):
        def project(left, part):
            columns = pl.ds(1024 * part, 1024)
            pltpu.make_async_copy(
                own_ref.at[:, columns], weights.at[section, :, columns], sems.at[section, part]
            ).wait()
            right = weights[section, :, 1024 * part : 1024 * (part + 1)]
            return jnp.dot(left, right, preferred_element_type=F32)

        return project

    return of_section(0), of_section(1)


def inside(pos, bands, table, token):
    window = table[pos[0]]
    row = first_row(window) + lax.rem(lax.div(token, WIN_COLS), WIN_ROWS)
    return (window >= 0) & (row >= 0) & (row < 3 * bands.shape[0] // 2)


def key_bias(pos, bands, table):
    token = lax.broadcasted_iota(jnp.int32, (1, WTOK), 1)
    return jnp.where(inside(pos, bands, table, token), 0.0, -1e30)


def early_kernel(
    pos, bands, table, raw_ref, far_ref, embed_ref, level_ref, gain_ref, own_ref, other_ref,
    hidden_ref, weights, sems,
):
    first, second = projections(pos, own_ref, other_ref, weights, sems)
    to_token = lax.broadcasted_iota(jnp.int32, (WTOK, WTOK), 0)
    from_token = lax.broadcasted_iota(jnp.int32, (WTOK, WTOK), 1)
    half = WTOK // 2
    to_window = (lax.div(to_token, half) == lax.rem(from_token, LEV)) & (
        lax.rem(to_token, half) == lax.div(from_token, LEV)
    )
    to_window = to_window.astype(BF)
    raws = [jnp.dot(to_window, ref[...], preferred_element_type=F32) for ref in (raw_ref, far_ref)]
    raw = jnp.concatenate(raws, axis=0).astype(BF)
    token = lax.broadcasted_iota(jnp.int32, (2 * WTOK, 1), 0)
    upper = lax.rem(token, WTOK) < half
    level_rows = jnp.where(upper, level_ref[0:1].astype(F32), level_ref[1:2].astype(F32))
    hidden = (jnp.dot(raw, embed_ref[...], preferred_element_type=F32) + level_rows).astype(BF)
    hidden = column_block(hidden, gain_ref[0:1], first)
    hidden_ref[...] = window_block(hidden, gain_ref[1:2], second, key_bias(pos, bands, table))


def late_kernel(
    pos, bands, table, came_ref, gain_ref, head_ref, own_ref, other_ref,
    give_ref, out_ref, rows_ref, weights, sems,
):
    first, second = projections(pos, own_ref, other_ref, weights, sems)
    hidden = window_block(came_ref[...], gain_ref[0:1], first, key_bias(pos, bands, table))
    hidden = column_block(hidden, gain_ref[1:2], second)
    result = jnp.dot(hidden, head_ref[...], preferred_element_type=F32)
    keep = inside(pos, bands, table, lax.broadcasted_iota(jnp.int32, (WTOK, 1), 0))
    to_token = lax.broadcasted_iota(jnp.int32, (WTOK, WTOK), 0)
    from_token = lax.broadcasted_iota(jnp.int32, (WTOK, WTOK), 1)
    half = WTOK // 2
    from_window = (lax.rem(to_token, LEV) == lax.div(from_token, half)) & (
        lax.div(to_token, LEV) == lax.rem(from_token, half)
    )
    from_window = from_window.astype(BF)
    for slab in range(2):
        out = jnp.where(keep, result[WTOK * slab : WTOK * (slab + 1)], 0.0).astype(BF)
        rows = jnp.dot(from_window, out, preferred_element_type=F32).astype(BF)
        if slab == 0:
            give_ref[0], give_ref[1] = out, rows
        else:
            out_ref[...], rows_ref[...] = out, rows


def sections_call(body, shapes, scalars, values, own, other, name):
    return pl.pallas_call(
        body,
        out_shape=tuple(jax.ShapeDtypeStruct(shape, BF) for shape in shapes),
        in_specs=[SMEM] * len(scalars) + [VMEM] * len(values) + [ANY] * 2,
        out_specs=(VMEM,) * len(shapes),
        scratch_shapes=[
            pltpu.VMEM((2, 1024, 4096), BF),
            pltpu.SemaphoreType.DMA((2, 4)),
        ],
        compiler_params=pltpu.CompilerParams(vmem_limit_bytes=60 * MIB),
        name=name,
    )(*scalars, *values, own, other)


def small_call(body, out_rows, scalars, value, name):
    return pl.pallas_call(
        body,
        out_shape=jax.ShapeDtypeStruct((out_rows, PACK, 128), BF),
        in_specs=[SMEM] * len(scalars) + [VMEM],
        out_specs=VMEM,
        name=name,
    )(*scalars, value)


def crossed(value, sources):
    return lax.ppermute(value, ("xh", "xl"), [(x, 3 - x) for x in sources])


def per_device(
    fields, band_rows, window_table, level_embed, embed_weight, attn_weight, norm_gain, head_weight
):
    late, core = lax.axis_index("xh"), lax.axis_index("c")
    is_late = late == 1
    pos = jnp.stack([lax.axis_index(LAT), lax.axis_index("z"), lax.axis_index("y"), core, late])
    lat_count = band_rows.shape[0]
    width = embed_weight.shape[1]
    turned = window_table.reshape(-1, 2)[:, ::-1].reshape(-1)
    table = jnp.where(is_late, turned, window_table)
    scalars = (pos, band_rows, table)

    message = small_call(pack_kernel, 2 * lat_count, (table,), to_rows(fields[0]), "pack")
    arrived = lax.all_to_all(message, LAT, 0, 0, tiled=True)
    gains = lax.all_gather(norm_gain, "c", axis=0, tiled=True)
    own, arrived, gains = gather_section(attn_weight, pos, message, arrived, gains)
    raw_rows = small_call(pick_kernel, WIN_ROWS + 1, scalars, arrived, "pick")
    own_raw = from_rows(raw_rows[:WIN_ROWS])
    far_raw = crossed(own_raw, (2, 3))
    other = swap(own, "c", 1)

    [hidden] = sections_call(
        early_kernel,
        [(2 * WTOK, width)],
        scalars,
        (own_raw, far_raw, embed_weight, level_embed, gains),
        own,
        other,
        "early",
    )
    came = crossed(hidden, (0, 1))
    given, out, rows = sections_call(
        late_kernel,
        [(2, WTOK, FEAT), (WTOK, FEAT), (WTOK, FEAT)],
        scalars,
        (came, gains, head_weight),
        own,
        other,
        "late",
    )
    taken = crossed(given, (2, 3))
    own_rows = jnp.where(is_late, rows, taken[1])
    reply = small_call(unpick_kernel, 2 * lat_count, scalars, to_rows(own_rows), "unpick")
    came_back = lax.all_to_all(reply, LAT, 0, 0, tiled=True)
    window_decoded = jnp.where(is_late, swap(out, "xl", 1), taken[0])[None]
    decoded_rows = small_call(unpack_kernel, 2 * LW + 1, scalars, came_back, "unpack")
    decoded = from_rows(decoded_rows[: 2 * LW])[None]
    return (decoded, window_decoded)


def solution(mesh):
    fine = Mesh(mesh.devices.reshape(2, 2, 8, 8, 2), ("xh", "c", "z", "y", "xl"))
    segment = ("xh", "c")
    placed = (
        P(segment, LAT, None),
        P(),
        P(),
        P(),
        P(),
        P(segment, None, LAT),
        P(segment, None),
        P(),
    )
    return jax.shard_map(
        per_device,
        mesh=fine,
        in_specs=placed,
        out_specs=(P(segment, LAT, None), P(segment, LAT, None)),
        check_vma=False,
    )
```

```python
import math

import jax
import jax.numpy as jnp
from jax import lax
from jax.experimental import pallas as pl
from jax.experimental.pallas import tpu as pltpu
from jax.sharding import Mesh
from jax.sharding import PartitionSpec as P

HEAD_DIM = 64
LEV = 2
WIN_ROWS = 12
WIN_COLS = 6
WTOK = 144
FEAT = 144
LW = 7
PIECE = WIN_COLS * LEV * FEAT
PACK = 16
BF = jnp.bfloat16
F32 = jnp.float32
LAT = ("z", "y", "xl")
DOUBLING = (4, 2, 1)
OFFS = (0, 4, 2, 6, 1, 5, 3, 7)
MIB = 1 << 20

VMEM = pl.BlockSpec(memory_space=pltpu.VMEM)
SMEM = pl.BlockSpec(memory_space=pltpu.SMEM)
ANY = pl.BlockSpec(memory_space=pl.ANY)


def ring(value, axis, by):
    n = lax.axis_size(axis)
    return lax.ppermute(value, axis, [(i, (i + by) % n) for i in range(n)])


def swap(value, axis, bit):
    n = lax.axis_size(axis)
    return lax.ppermute(value, axis, [(i, i ^ bit) for i in range(n)])


def seventh(window):
    return lax.shift_right_logical(window * 147, 10)


def first_row(window):
    return WIN_ROWS * seventh(jnp.maximum(window, 0)) - WIN_ROWS // 2


def pack_kernel(table, rows_ref, out_ref):
    def shard(j, carry):
        window = jnp.maximum(table[j], 0)
        column = window - LW * seventh(window)
        out_ref[2 * j] = rows_ref[column]
        out_ref[2 * j + 1] = rows_ref[LW + column]
        return carry

    lax.fori_loop(0, table.shape[0], shard, 0, unroll=8)


def pick_kernel(where, bands, table, came_ref, out_ref):
    window = table[where[0]]
    first = first_row(window)
    out_ref[...] = jnp.zeros_like(out_ref)
    count_rows = jnp.where(window >= 0, WIN_ROWS, 0)

    def band(i, row):
        count = bands[i]
        here = (row >= 0) & (row < count_rows)
        out_ref[jnp.where(here, row, WIN_ROWS)] = came_ref[2 * i]
        here = (count > 1) & (row >= -1) & (row + 1 < count_rows)
        out_ref[jnp.where(here, row + 1, WIN_ROWS)] = came_ref[2 * i + 1]
        return row + count

    lax.fori_loop(0, bands.shape[0], band, -first, unroll=8)


def unpick_kernel(where, bands, table, rows_ref, out_ref):
    first = first_row(table[where[0]])

    def band(i, row):
        out_ref[2 * i] = rows_ref[jnp.clip(row, 0, WIN_ROWS - 1)]
        out_ref[2 * i + 1] = rows_ref[jnp.clip(row + 1, 0, WIN_ROWS - 1)]
        return row + bands[i]

    lax.fori_loop(0, bands.shape[0], band, -first, unroll=8)


def unpack_kernel(where, bands, table, came_ref, out_ref):
    mine = where[0]
    start = lax.fori_loop(
        0, bands.shape[0], lambda i, total: total + jnp.where(i < mine, bands[i], 0), jnp.int32(0), unroll=8
    )
    across = lax.div(start + WIN_ROWS // 2, WIN_ROWS)
    across_next = jnp.where(bands[mine] > 1, lax.div(start + 1 + WIN_ROWS // 2, WIN_ROWS), -1)
    out_ref[...] = jnp.zeros_like(out_ref)

    def shard(j, carry):
        window = jnp.maximum(table[j], 0)
        line = jnp.where(table[j] >= 0, seventh(window), -2)
        column = window - LW * seventh(window)
        out_ref[jnp.where(line == across, column, 2 * LW)] = came_ref[2 * j]
        out_ref[jnp.where(line == across_next, LW + column, 2 * LW)] = came_ref[2 * j + 1]
        return carry

    lax.fori_loop(0, table.shape[0], shard, 0, unroll=8)


def to_rows(tokens):
    rows = tokens.reshape(-1, PIECE)
    return jnp.pad(rows, ((0, 0), (0, PACK * 128 - PIECE))).reshape(-1, PACK, 128)


def from_rows(rows):
    return rows.reshape(-1, PACK * 128)[:, :PIECE].reshape(-1, FEAT)


def join_kernel(pos, *refs):
    out_ref, held, turned, sems, sent = refs[-5:]
    pieces = refs[:-5]
    half = len(pieces) // 2
    z, y = pos[1], pos[2]
    steps = (0, -1, -2, -3, 1, 2, 3, 4)

    def copies(side, index):
        ref = pieces[side * half + index]
        for sub in range(8):
            if side == 0:
                plane, line = lax.rem(z + steps[index] + 8, 8), y ^ OFFS[sub]
            else:
                plane, line = z ^ OFFS[sub], lax.rem(y + steps[index] + 8, 8)
            row = pl.multiple_of((plane * 8 + line) * 64, 64)
            yield pltpu.make_async_copy(
                ref.at[pl.ds(sub * 64, 64)], held.at[side, pl.ds(row, 64)], sems.at[side, index]
            )

    def turn(side, plane):
        columns = pl.ds(pl.multiple_of(plane * 512, 512), 512)
        here = (slice(512 * side, 512 * (side + 1)), columns)
        turned[here] = held[side, columns, :].T
        copy = pltpu.make_async_copy(turned.at[here], out_ref.at[here], sent)
        copy.start()
        return copy

    every = [[list(copies(side, index)) for index in range(half)] for side in range(2)]
    for side in range(2):
        for group in every[side]:
            for c in group:
                c.start()
    leaving = []
    for index in range(half):
        for c in every[0][index]:
            c.wait()
        leaving.append(turn(0, lax.rem(z + steps[index] + 8, 8)))
    for group in every[1]:
        for c in group:
            c.wait()
    for plane in range(8):
        leaving.append(turn(1, plane))
    for c in leaving:
        c.wait()


def gather_section(weight, pos, message, gains):
    mine = weight[0].T
    pair = lax.all_gather(mine, "xl", axis=0, tiled=True)
    pair, gains = lax.optimization_barrier((pair, gains))
    a, b = pair[:, :512], pair[:, 512:]
    for bit in DOUBLING:
        a_far, b_far = swap(a, "y", bit), swap(b, "z", bit)
        a, b = jnp.concatenate([a, a_far]), jnp.concatenate([b, b_far])
    chains = [("z", 1), ("z", -1), ("y", 1), ("y", -1)]
    got = [[] for _ in chains]
    held = [a, a, b, b]
    for step in range(4):
        for n, (axis, by) in enumerate(chains):
            if step < 3 or by > 0:
                held[n] = ring(held[n], axis, by)
                got[n].append(held[n])
    *lasts, message = lax.optimization_barrier((*[g[-1] for g in got], message))
    for g, last in zip(got, lasts):
        g[-1] = last
    pieces = []
    for own, ahead, behind in ((a, got[0], got[1]), (b, got[2], got[3])):
        pieces += [own, *ahead[:3], *behind, ahead[3]]
    section = pl.pallas_call(
        join_kernel,
        out_shape=jax.ShapeDtypeStruct((1024, 4096), BF),
        in_specs=[SMEM] + [ANY] * len(pieces),
        out_specs=ANY,
        scratch_shapes=[
            pltpu.VMEM((2, 4096, 512), BF),
            pltpu.VMEM((1024, 4096), BF),
            pltpu.SemaphoreType.DMA((2, 8)),
            pltpu.SemaphoreType.DMA(()),
        ],
        compiler_params=pltpu.CompilerParams(vmem_limit_bytes=60 * MIB),
        cost_estimate=pl.CostEstimate(flops=10**10, bytes_accessed=3 << 23, transcendentals=0),
        name="join",
    )(pos, *pieces)
    return section, message, gains


def matmul_t(left, right):
    return lax.dot_general(left, right, (((1,), (1,)), ((), ())), preferred_element_type=F32)


def normed_of(wide, gain):
    scale = lax.rsqrt(jnp.mean(wide * wide, axis=-1, keepdims=True) + 1e-06)
    return (wide * scale * gain).astype(BF)


def other_level(value):
    half = WTOK // 2
    parts = [value[half * i : half * (i + 1)] for i in range(value.shape[0] // half)]
    return jnp.concatenate([parts[i ^ 1] for i in range(len(parts))], axis=0)


def column_block(hidden, gain, project):
    wide = hidden.astype(F32)
    normed = normed_of(wide, gain)
    query = project(normed, 0).astype(BF).astype(F32)
    keyed = project(normed, 1).astype(BF).astype(F32)
    product = query * (keyed - other_level(keyed))
    lane = lax.broadcasted_iota(jnp.int32, (1024, 128), 0)
    head = lax.broadcasted_iota(jnp.int32, (1024, 128), 1)
    of_head = (lax.div(lane, HEAD_DIM) == head).astype(BF)
    high = product.astype(BF)
    low = (product - high.astype(F32)).astype(BF)
    gap = (
        jnp.dot(high, of_head, preferred_element_type=F32)
        + jnp.dot(low, of_head, preferred_element_type=F32)
    ) * (1 / math.sqrt(HEAD_DIM))
    small = jnp.exp(-jnp.abs(gap))
    larger = 1.0 / (1.0 + small)
    smaller = small * larger
    own = jnp.where(gap >= 0, larger, smaller).astype(BF)
    far = jnp.where(gap >= 0, smaller, larger).astype(BF)
    valued = project(normed, 2).astype(BF).astype(F32)
    mixed = (matmul_t(own, of_head) * valued + matmul_t(far, of_head) * other_level(valued)).astype(BF)
    return (wide + project(mixed, 3)).astype(BF)


def window_block(hidden, gain, project, bias):
    wide = hidden.astype(F32)
    normed = normed_of(wide, gain)
    query = (project(normed, 0).astype(BF).astype(F32) * (1 / math.sqrt(HEAD_DIM))).astype(BF)
    keyed = project(normed, 1).astype(BF)
    valued = project(normed, 2).astype(BF)
    low = lax.broadcasted_iota(jnp.int32, (WTOK, 128), 1) < HEAD_DIM
    ones = jnp.ones((WTOK, 128), BF)
    slabs = []
    for slab in range(hidden.shape[0] // WTOK):
        here = slice(WTOK * slab, WTOK * (slab + 1))
        mixed = []
        for two in range(8):
            lanes = slice(128 * two, 128 * (two + 1))
            q2, k2 = query[here, lanes], keyed[here, lanes]
            v2 = jnp.concatenate([valued[here, lanes], ones], axis=1)
            outs = []
            for part in range(2):
                q1 = jnp.where(low if part == 0 else ~low, q2, jnp.zeros_like(q2))
                scores = matmul_t(q1, k2) + bias
                top = jnp.max(scores, axis=-1, keepdims=True)
                grown = jnp.exp(scores - top).astype(BF)
                summed = jnp.dot(grown, v2, preferred_element_type=F32)
                outs.append(summed[:, :128] / summed[:, 128:])
            mixed.append(jnp.where(low, outs[0], outs[1]).astype(BF))
        slabs.append(jnp.concatenate(mixed, axis=1))
    mixed = jnp.concatenate(slabs, axis=0)
    return (wide + project(mixed, 3)).astype(BF)


def projections(pos, own_ref, other_ref, weights, sems):
    core = pos[3]

    def load(source, section):
        for part in range(4):
            columns = pl.ds(1024 * part, 1024)
            pltpu.make_async_copy(
                source.at[:, columns], weights.at[section, :, columns], sems.at[section, part]
            ).start()

    @pl.when(core == 0)
    def _():
        load(own_ref, 0)
        load(other_ref, 1)

    @pl.when(core == 1)
    def _():
        load(other_ref, 0)
        load(own_ref, 1)

    def of_section(section):
        def project(left, part):
            columns = pl.ds(1024 * part, 1024)
            pltpu.make_async_copy(
                own_ref.at[:, columns], weights.at[section, :, columns], sems.at[section, part]
            ).wait()
            right = weights[section, :, 1024 * part : 1024 * (part + 1)]
            return jnp.dot(left, right, preferred_element_type=F32)

        return project

    return of_section(0), of_section(1)


def inside(pos, bands, table, token):
    window = table[pos[0]]
    row = first_row(window) + lax.rem(lax.div(token, WIN_COLS), WIN_ROWS)
    return (window >= 0) & (row >= 0) & (row < 3 * bands.shape[0] // 2)


def key_bias(pos, bands, table):
    token = lax.broadcasted_iota(jnp.int32, (1, WTOK), 1)
    return jnp.where(inside(pos, bands, table, token), 0.0, -1e30)


def early_kernel(
    pos, bands, table, raw_ref, embed_ref, level_ref, gain_ref, own_ref, other_ref,
    hidden_ref, weights, sems,
):
    first, second = projections(pos, own_ref, other_ref, weights, sems)
    to_token = lax.broadcasted_iota(jnp.int32, (WTOK, WTOK), 0)
    from_token = lax.broadcasted_iota(jnp.int32, (WTOK, WTOK), 1)
    half = WTOK // 2
    to_window = (lax.div(to_token, half) == lax.rem(from_token, LEV)) & (
        lax.rem(to_token, half) == lax.div(from_token, LEV)
    )
    raw = jnp.dot(to_window.astype(BF), raw_ref[...], preferred_element_type=F32).astype(BF)
    upper = lax.broadcasted_iota(jnp.int32, (WTOK, 1), 0) < half
    level_rows = jnp.where(upper, level_ref[0:1].astype(F32), level_ref[1:2].astype(F32))
    embedded = (jnp.dot(raw, embed_ref[...], preferred_element_type=F32) + level_rows).astype(BF)
    hidden = column_block(embedded, gain_ref[0:1], first)
    hidden_ref[...] = window_block(hidden, gain_ref[1:2], second, key_bias(pos, bands, table))


def late_kernel(
    pos, bands, table, came_ref, came_too_ref, gain_ref, head_ref, own_ref, other_ref,
    give_ref, out_ref, rows_ref, weights, sems,
):
    first, second = projections(pos, own_ref, other_ref, weights, sems)
    start = jnp.concatenate([came_ref[...], came_too_ref[...]], axis=0)
    hidden = window_block(start, gain_ref[0:1], first, key_bias(pos, bands, table))
    hidden = column_block(hidden, gain_ref[1:2], second)
    result = jnp.dot(hidden, head_ref[...], preferred_element_type=F32)
    keep = inside(pos, bands, table, lax.broadcasted_iota(jnp.int32, (WTOK, 1), 0))
    to_token = lax.broadcasted_iota(jnp.int32, (WTOK, WTOK), 0)
    from_token = lax.broadcasted_iota(jnp.int32, (WTOK, WTOK), 1)
    half = WTOK // 2
    from_window = (lax.rem(to_token, LEV) == lax.div(from_token, half)) & (
        lax.div(to_token, LEV) == lax.rem(from_token, half)
    )
    from_window = from_window.astype(BF)
    for slab in range(2):
        out = jnp.where(keep, result[WTOK * slab : WTOK * (slab + 1)], 0.0).astype(BF)
        rows = jnp.dot(from_window, out, preferred_element_type=F32).astype(BF)
        if slab == 0:
            give_ref[0], give_ref[1] = out, rows
        else:
            out_ref[...], rows_ref[...] = out, rows


def sections_call(body, shapes, scalars, values, own, other, name):
    return pl.pallas_call(
        body,
        out_shape=tuple(jax.ShapeDtypeStruct(shape, BF) for shape in shapes),
        in_specs=[SMEM] * len(scalars) + [VMEM] * len(values) + [ANY] * 2,
        out_specs=(VMEM,) * len(shapes),
        scratch_shapes=[
            pltpu.VMEM((2, 1024, 4096), BF),
            pltpu.SemaphoreType.DMA((2, 4)),
        ],
        compiler_params=pltpu.CompilerParams(vmem_limit_bytes=60 * MIB),
        name=name,
    )(*scalars, *values, own, other)


def small_call(body, out_rows, scalars, value, name):
    return pl.pallas_call(
        body,
        out_shape=jax.ShapeDtypeStruct((out_rows, PACK, 128), BF),
        in_specs=[SMEM] * len(scalars) + [VMEM],
        out_specs=VMEM,
        name=name,
    )(*scalars, value)


def crossed(value, sources):
    return lax.ppermute(value, ("xh", "xl"), [(x, 3 - x) for x in sources])


def per_device(
    fields, band_rows, window_table, level_embed, embed_weight, attn_weight, norm_gain, head_weight
):
    late, core = lax.axis_index("xh"), lax.axis_index("c")
    is_late = late == 1
    pos = jnp.stack([lax.axis_index(LAT), lax.axis_index("z"), lax.axis_index("y"), core, late])
    lat_count = band_rows.shape[0]
    width = embed_weight.shape[1]
    turned = window_table.reshape(-1, 2)[:, ::-1].reshape(-1)
    table = jnp.where(is_late, turned, window_table)
    scalars = (pos, band_rows, table)

    message = small_call(pack_kernel, 2 * lat_count, (table,), to_rows(fields[0]), "pack")
    gains = lax.all_gather(norm_gain, "c", axis=0, tiled=True)
    own, message, gains = gather_section(attn_weight, pos, message, gains)
    arrived = lax.all_to_all(message, LAT, 0, 0, tiled=True)
    other = swap(own, "c", 1)
    raw_rows = small_call(pick_kernel, WIN_ROWS + 1, scalars, arrived, "pick")
    own_raw = from_rows(raw_rows[:WIN_ROWS])
    far_raw = crossed(own_raw, (2, 3))

    came = []
    for raw in (own_raw, far_raw):
        [hidden] = sections_call(
            early_kernel,
            [(WTOK, width)],
            scalars,
            (raw, embed_weight, level_embed, gains),
            own,
            other,
            "early",
        )
        came.append(crossed(hidden, (0, 1)))
    given, out, rows = sections_call(
        late_kernel,
        [(2, WTOK, FEAT), (WTOK, FEAT), (WTOK, FEAT)],
        scalars,
        (*came, gains, head_weight),
        own,
        other,
        "late",
    )
    taken = crossed(given, (2, 3))
    own_rows = jnp.where(is_late, rows, taken[1])
    reply = small_call(unpick_kernel, 2 * lat_count, scalars, to_rows(own_rows), "unpick")
    came_back = lax.all_to_all(reply, LAT, 0, 0, tiled=True)
    window_decoded = jnp.where(is_late, swap(out, "xl", 1), taken[0])[None]
    decoded_rows = small_call(unpack_kernel, 2 * LW + 1, scalars, came_back, "unpack")
    decoded = from_rows(decoded_rows[: 2 * LW])[None]
    return (decoded, window_decoded)


def solution(mesh):
    fine = Mesh(mesh.devices.reshape(2, 2, 8, 8, 2), ("xh", "c", "z", "y", "xl"))
    segment = ("xh", "c")
    placed = (
        P(segment, LAT, None),
        P(),
        P(),
        P(),
        P(),
        P(segment, None, LAT),
        P(segment, None),
        P(),
    )
    return jax.shard_map(
        per_device,
        mesh=fine,
        in_specs=placed,
        out_specs=(P(segment, LAT, None), P(segment, LAT, None)),
        check_vma=False,
    )
```

```python
import math

import jax
import jax.numpy as jnp
from jax import lax
from jax.experimental import pallas as pl
from jax.experimental.pallas import tpu as pltpu
from jax.sharding import Mesh
from jax.sharding import PartitionSpec as P

HEAD_DIM = 64
LEV = 2
WIN_ROWS = 12
WIN_COLS = 6
WTOK = 144
FEAT = 144
LW = 7
PIECE = WIN_COLS * LEV * FEAT
PACK = 16
BF = jnp.bfloat16
F32 = jnp.float32
LAT = ("z", "y", "xl")
DOUBLING = (4, 2, 1)
OFFS = (0, 4, 2, 6, 1, 5, 3, 7)
MIB = 1 << 20

VMEM = pl.BlockSpec(memory_space=pltpu.VMEM)
SMEM = pl.BlockSpec(memory_space=pltpu.SMEM)
ANY = pl.BlockSpec(memory_space=pl.ANY)


def ring(value, axis, by):
    n = lax.axis_size(axis)
    return lax.ppermute(value, axis, [(i, (i + by) % n) for i in range(n)])


def swap(value, axis, bit):
    n = lax.axis_size(axis)
    return lax.ppermute(value, axis, [(i, i ^ bit) for i in range(n)])


def seventh(window):
    return lax.shift_right_logical(window * 147, 10)


def first_row(window):
    return WIN_ROWS * seventh(jnp.maximum(window, 0)) - WIN_ROWS // 2


def pack_kernel(where, bands, table, rows_ref, out_ref):
    column_of_bands, z = lax.rem(where[0], 16), where[1]
    starts, blocks = [], []
    total = jnp.int32(0)
    for far in range(bands.shape[0] // 16):
        def add(i, sums, base=16 * far):
            count = bands[base + i]
            return sums[0] + count, sums[1] + jnp.where(i < column_of_bands, count, 0)

        total, start = lax.fori_loop(0, 16, add, (total, total), unroll=4)
        starts.append(start)
        step = z ^ far
        place = (lax.rem(step, 2) * 4) | (step & 2) | lax.div(step, 4)
        blocks.append(place * 2 * LW)
    for shard in range(16):
        window = jnp.maximum(table[z * 16 + shard], 0)
        first = first_row(window)
        block = jnp.int32(0)
        for start, at in zip(starts, blocks):
            row = start - first
            block = jnp.where((row >= -1) & (row < WIN_ROWS), at, block)
        column = block + window - LW * seventh(window)
        out_ref[2 * shard] = rows_ref[column]
        out_ref[2 * shard + 1] = rows_ref[LW + column]


def pick_kernel(where, bands, table, came_ref, out_ref):
    window = table[where[0]]
    first = first_row(window)
    out_ref[...] = jnp.zeros_like(out_ref)
    count_rows = jnp.where(window >= 0, WIN_ROWS, 0)

    def band(i, row):
        count = bands[i]
        here = (row >= 0) & (row < count_rows)
        out_ref[jnp.where(here, row, WIN_ROWS)] = came_ref[2 * (i & 15)]
        here = (count > 1) & (row >= -1) & (row + 1 < count_rows)
        out_ref[jnp.where(here, row + 1, WIN_ROWS)] = came_ref[2 * (i & 15) + 1]
        return row + count

    lax.fori_loop(0, bands.shape[0], band, -first, unroll=8)


def unpick_kernel(where, bands, table, rows_ref, out_ref):
    first = first_row(table[where[0]])

    def band(i, row):
        out_ref[2 * i] = rows_ref[jnp.clip(row, 0, WIN_ROWS - 1)]
        out_ref[2 * i + 1] = rows_ref[jnp.clip(row + 1, 0, WIN_ROWS - 1)]
        return row + bands[i]

    lax.fori_loop(0, bands.shape[0], band, -first, unroll=8)


def unpack_kernel(where, bands, table, came_ref, out_ref):
    mine = where[0]
    start = lax.fori_loop(
        0, bands.shape[0], lambda i, total: total + jnp.where(i < mine, bands[i], 0), jnp.int32(0), unroll=8
    )
    across = lax.div(start + WIN_ROWS // 2, WIN_ROWS)
    across_next = jnp.where(bands[mine] > 1, lax.div(start + 1 + WIN_ROWS // 2, WIN_ROWS), -1)
    out_ref[...] = jnp.zeros_like(out_ref)

    def shard(j, carry):
        window = jnp.maximum(table[j], 0)
        line = jnp.where(table[j] >= 0, seventh(window), -2)
        column = window - LW * seventh(window)
        out_ref[jnp.where(line == across, column, 2 * LW)] = came_ref[2 * j]
        out_ref[jnp.where(line == across_next, LW + column, 2 * LW)] = came_ref[2 * j + 1]
        return carry

    lax.fori_loop(0, table.shape[0], shard, 0, unroll=8)


def to_rows(tokens):
    rows = tokens.reshape(-1, PIECE)
    return jnp.pad(rows, ((0, 0), (0, PACK * 128 - PIECE))).reshape(-1, PACK, 128)


def from_rows(rows):
    return rows.reshape(-1, PACK * 128)[:, :PIECE].reshape(-1, FEAT)


def join_kernel(pos, *refs):
    out_ref, held, turned, sems, sent = refs[-5:]
    pieces = refs[:-5]
    half = len(pieces) // 2
    z, y = pos[1], pos[2]
    steps = (0, -1, -2, -3, 1, 2, 3, 4)

    def copies(side, index):
        ref = pieces[side * half + index]
        for sub in range(8):
            if side == 0:
                plane, line = lax.rem(z + steps[index] + 8, 8), y ^ OFFS[sub]
            else:
                plane, line = z ^ OFFS[sub], lax.rem(y + steps[index] + 8, 8)
            row = pl.multiple_of((plane * 8 + line) * 64, 64)
            yield pltpu.make_async_copy(
                ref.at[pl.ds(sub * 64, 64)], held.at[side, pl.ds(row, 64)], sems.at[side, index]
            )

    def turn(side, plane):
        columns = pl.ds(pl.multiple_of(plane * 512, 512), 512)
        here = (slice(512 * side, 512 * (side + 1)), columns)
        turned[here] = held[side, columns, :].T
        copy = pltpu.make_async_copy(turned.at[here], out_ref.at[here], sent)
        copy.start()
        return copy

    every = [[list(copies(side, index)) for index in range(half)] for side in range(2)]
    for side in range(2):
        for group in every[side]:
            for c in group:
                c.start()
    leaving = []
    for index in range(half):
        for c in every[0][index]:
            c.wait()
        leaving.append(turn(0, lax.rem(z + steps[index] + 8, 8)))
    for group in every[1]:
        for c in group:
            c.wait()
    for plane in range(8):
        leaving.append(turn(1, plane))
    for c in leaving:
        c.wait()


def gather_section(weight, pos, rows, gains, pack):
    mine = weight[0].T
    pair = lax.all_gather(mine, "xl", axis=0, tiled=True)
    pair, gains = lax.optimization_barrier((pair, gains))
    a, b = pair[:, :512], pair[:, 512:]
    for bit in DOUBLING:
        a_far, b_far = swap(a, "y", bit), swap(b, "z", bit)
        a, b = jnp.concatenate([a, a_far]), jnp.concatenate([b, b_far])
    for bit in DOUBLING:
        rows = jnp.concatenate([rows, swap(rows, "z", bit)])
    a, b, rows = lax.optimization_barrier((a, b, rows))
    message = pack(rows)
    chains = [("z", 1), ("z", -1), ("y", 1), ("y", -1)]
    got = [[] for _ in chains]
    held = [a, a, b, b]
    for step in range(4):
        for n, (axis, by) in enumerate(chains):
            if step < 3 or by > 0:
                held[n] = ring(held[n], axis, by)
                got[n].append(held[n])
    *lasts, message = lax.optimization_barrier((*[g[-1] for g in got], message))
    for g, last in zip(got, lasts):
        g[-1] = last
    pieces = []
    for own, ahead, behind in ((a, got[0], got[1]), (b, got[2], got[3])):
        pieces += [own, *ahead[:3], *behind, ahead[3]]
    section = pl.pallas_call(
        join_kernel,
        out_shape=jax.ShapeDtypeStruct((1024, 4096), BF),
        in_specs=[SMEM] + [ANY] * len(pieces),
        out_specs=ANY,
        scratch_shapes=[
            pltpu.VMEM((2, 4096, 512), BF),
            pltpu.VMEM((1024, 4096), BF),
            pltpu.SemaphoreType.DMA((2, 8)),
            pltpu.SemaphoreType.DMA(()),
        ],
        compiler_params=pltpu.CompilerParams(vmem_limit_bytes=60 * MIB),
        cost_estimate=pl.CostEstimate(flops=10**10, bytes_accessed=3 << 23, transcendentals=0),
        name="join",
    )(pos, *pieces)
    return section, message, gains


def matmul_t(left, right):
    return lax.dot_general(left, right, (((1,), (1,)), ((), ())), preferred_element_type=F32)


def normed_of(wide, gain):
    scale = lax.rsqrt(jnp.mean(wide * wide, axis=-1, keepdims=True) + 1e-06)
    return (wide * scale * gain).astype(BF)


def other_level(value):
    half = WTOK // 2
    parts = [value[half * i : half * (i + 1)] for i in range(value.shape[0] // half)]
    return jnp.concatenate([parts[i ^ 1] for i in range(len(parts))], axis=0)


def column_block(hidden, gain, project):
    wide = hidden.astype(F32)
    normed = normed_of(wide, gain)
    query = project(normed, 0).astype(BF).astype(F32)
    keyed = project(normed, 1).astype(BF).astype(F32)
    product = query * (keyed - other_level(keyed))
    lane = lax.broadcasted_iota(jnp.int32, (1024, 128), 0)
    head = lax.broadcasted_iota(jnp.int32, (1024, 128), 1)
    of_head = (lax.div(lane, HEAD_DIM) == head).astype(BF)
    high = product.astype(BF)
    low = (product - high.astype(F32)).astype(BF)
    gap = (
        jnp.dot(high, of_head, preferred_element_type=F32)
        + jnp.dot(low, of_head, preferred_element_type=F32)
    ) * (1 / math.sqrt(HEAD_DIM))
    small = jnp.exp(-jnp.abs(gap))
    larger = 1.0 / (1.0 + small)
    smaller = small * larger
    own = jnp.where(gap >= 0, larger, smaller).astype(BF)
    far = jnp.where(gap >= 0, smaller, larger).astype(BF)
    valued = project(normed, 2).astype(BF).astype(F32)
    mixed = (matmul_t(own, of_head) * valued + matmul_t(far, of_head) * other_level(valued)).astype(BF)
    return (wide + project(mixed, 3)).astype(BF)


def window_block(hidden, gain, project, bias):
    wide = hidden.astype(F32)
    normed = normed_of(wide, gain)
    query = (project(normed, 0).astype(BF).astype(F32) * (1 / math.sqrt(HEAD_DIM))).astype(BF)
    keyed = project(normed, 1).astype(BF)
    valued = project(normed, 2).astype(BF)
    low = lax.broadcasted_iota(jnp.int32, (WTOK, 128), 1) < HEAD_DIM
    ones = jnp.ones((WTOK, 128), BF)
    slabs = []
    for slab in range(hidden.shape[0] // WTOK):
        here = slice(WTOK * slab, WTOK * (slab + 1))
        mixed = []
        for two in range(8):
            lanes = slice(128 * two, 128 * (two + 1))
            q2, k2 = query[here, lanes], keyed[here, lanes]
            v2 = jnp.concatenate([valued[here, lanes], ones], axis=1)
            outs = []
            for part in range(2):
                q1 = jnp.where(low if part == 0 else ~low, q2, jnp.zeros_like(q2))
                scores = matmul_t(q1, k2) + bias
                top = jnp.max(scores, axis=-1, keepdims=True)
                grown = jnp.exp(scores - top).astype(BF)
                summed = jnp.dot(grown, v2, preferred_element_type=F32)
                outs.append(summed[:, :128] / summed[:, 128:])
            mixed.append(jnp.where(low, outs[0], outs[1]).astype(BF))
        slabs.append(jnp.concatenate(mixed, axis=1))
    mixed = jnp.concatenate(slabs, axis=0)
    return (wide + project(mixed, 3)).astype(BF)


def projections(pos, own_ref, other_ref, weights, sems):
    core = pos[3]

    def load(source, section):
        for part in range(4):
            columns = pl.ds(1024 * part, 1024)
            pltpu.make_async_copy(
                source.at[:, columns], weights.at[section, :, columns], sems.at[section, part]
            ).start()

    @pl.when(core == 0)
    def _():
        load(own_ref, 0)
        load(other_ref, 1)

    @pl.when(core == 1)
    def _():
        load(other_ref, 0)
        load(own_ref, 1)

    def of_section(section):
        def project(left, part):
            columns = pl.ds(1024 * part, 1024)
            pltpu.make_async_copy(
                own_ref.at[:, columns], weights.at[section, :, columns], sems.at[section, part]
            ).wait()
            right = weights[section, :, 1024 * part : 1024 * (part + 1)]
            return jnp.dot(left, right, preferred_element_type=F32)

        return project

    return of_section(0), of_section(1)


def inside(pos, bands, table, token):
    window = table[pos[0]]
    row = first_row(window) + lax.rem(lax.div(token, WIN_COLS), WIN_ROWS)
    return (window >= 0) & (row >= 0) & (row < 3 * bands.shape[0] // 2)


def key_bias(pos, bands, table):
    token = lax.broadcasted_iota(jnp.int32, (1, WTOK), 1)
    return jnp.where(inside(pos, bands, table, token), 0.0, -1e30)


def early_kernel(
    pos, bands, table, raw_ref, embed_ref, level_ref, gain_ref, own_ref, other_ref,
    hidden_ref, weights, sems,
):
    first, second = projections(pos, own_ref, other_ref, weights, sems)
    to_token = lax.broadcasted_iota(jnp.int32, (WTOK, WTOK), 0)
    from_token = lax.broadcasted_iota(jnp.int32, (WTOK, WTOK), 1)
    half = WTOK // 2
    to_window = (lax.div(to_token, half) == lax.rem(from_token, LEV)) & (
        lax.rem(to_token, half) == lax.div(from_token, LEV)
    )
    raw = jnp.dot(to_window.astype(BF), raw_ref[...], preferred_element_type=F32).astype(BF)
    upper = lax.broadcasted_iota(jnp.int32, (WTOK, 1), 0) < half
    level_rows = jnp.where(upper, level_ref[0:1].astype(F32), level_ref[1:2].astype(F32))
    embedded = (jnp.dot(raw, embed_ref[...], preferred_element_type=F32) + level_rows).astype(BF)
    hidden = column_block(embedded, gain_ref[0:1], first)
    hidden_ref[...] = window_block(hidden, gain_ref[1:2], second, key_bias(pos, bands, table))


def late_kernel(
    pos, bands, table, came_ref, came_too_ref, gain_ref, head_ref, own_ref, other_ref,
    give_ref, out_ref, rows_ref, weights, sems,
):
    first, second = projections(pos, own_ref, other_ref, weights, sems)
    start = jnp.concatenate([came_ref[...], came_too_ref[...]], axis=0)
    hidden = window_block(start, gain_ref[0:1], first, key_bias(pos, bands, table))
    hidden = column_block(hidden, gain_ref[1:2], second)
    result = jnp.dot(hidden, head_ref[...], preferred_element_type=F32)
    keep = inside(pos, bands, table, lax.broadcasted_iota(jnp.int32, (WTOK, 1), 0))
    to_token = lax.broadcasted_iota(jnp.int32, (WTOK, WTOK), 0)
    from_token = lax.broadcasted_iota(jnp.int32, (WTOK, WTOK), 1)
    half = WTOK // 2
    from_window = (lax.rem(to_token, LEV) == lax.div(from_token, half)) & (
        lax.div(to_token, LEV) == lax.rem(from_token, half)
    )
    from_window = from_window.astype(BF)
    for slab in range(2):
        out = jnp.where(keep, result[WTOK * slab : WTOK * (slab + 1)], 0.0).astype(BF)
        rows = jnp.dot(from_window, out, preferred_element_type=F32).astype(BF)
        if slab == 0:
            give_ref[0], give_ref[1] = out, rows
        else:
            out_ref[...], rows_ref[...] = out, rows


def sections_call(body, shapes, scalars, values, own, other, name):
    return pl.pallas_call(
        body,
        out_shape=tuple(jax.ShapeDtypeStruct(shape, BF) for shape in shapes),
        in_specs=[SMEM] * len(scalars) + [VMEM] * len(values) + [ANY] * 2,
        out_specs=(VMEM,) * len(shapes),
        scratch_shapes=[
            pltpu.VMEM((2, 1024, 4096), BF),
            pltpu.SemaphoreType.DMA((2, 4)),
        ],
        compiler_params=pltpu.CompilerParams(vmem_limit_bytes=60 * MIB),
        name=name,
    )(*scalars, *values, own, other)


def small_call(body, out_rows, scalars, value, name):
    return pl.pallas_call(
        body,
        out_shape=jax.ShapeDtypeStruct((out_rows, PACK, 128), BF),
        in_specs=[SMEM] * len(scalars) + [VMEM],
        out_specs=VMEM,
        name=name,
    )(*scalars, value)


def crossed(value, sources):
    return lax.ppermute(value, ("xh", "xl"), [(x, 3 - x) for x in sources])


def per_device(
    fields, band_rows, window_table, level_embed, embed_weight, attn_weight, norm_gain, head_weight
):
    late, core = lax.axis_index("xh"), lax.axis_index("c")
    is_late = late == 1
    pos = jnp.stack([lax.axis_index(LAT), lax.axis_index("z"), lax.axis_index("y"), core, late])
    lat_count = band_rows.shape[0]
    width = embed_weight.shape[1]
    turned = window_table.reshape(-1, 2)[:, ::-1].reshape(-1)
    table = jnp.where(is_late, turned, window_table)
    scalars = (pos, band_rows, table)

    gains = lax.all_gather(norm_gain, "c", axis=0, tiled=True)
    own, message, gains = gather_section(
        attn_weight,
        pos,
        to_rows(fields[0]),
        gains,
        lambda rows: small_call(pack_kernel, 32, scalars, rows, "pack"),
    )
    arrived = lax.all_to_all(message, ("y", "xl"), 0, 0, tiled=True)
    other = swap(own, "c", 1)
    raw_rows = small_call(pick_kernel, WIN_ROWS + 1, scalars, arrived, "pick")
    own_raw = from_rows(raw_rows[:WIN_ROWS])
    far_raw = crossed(own_raw, (2, 3))

    came = []
    for raw in (own_raw, far_raw):
        [hidden] = sections_call(
            early_kernel,
            [(WTOK, width)],
            scalars,
            (raw, embed_weight, level_embed, gains),
            own,
            other,
            "early",
        )
        came.append(crossed(hidden, (0, 1)))
    given, out, rows = sections_call(
        late_kernel,
        [(2, WTOK, FEAT), (WTOK, FEAT), (WTOK, FEAT)],
        scalars,
        (*came, gains, head_weight),
        own,
        other,
        "late",
    )
    taken = crossed(given, (2, 3))
    own_rows = jnp.where(is_late, rows, taken[1])
    reply = small_call(unpick_kernel, 2 * lat_count, scalars, to_rows(own_rows), "unpick")
    came_back = lax.all_to_all(reply, LAT, 0, 0, tiled=True)
    window_decoded = jnp.where(is_late, swap(out, "xl", 1), taken[0])[None]
    decoded_rows = small_call(unpack_kernel, 2 * LW + 1, scalars, came_back, "unpack")
    decoded = from_rows(decoded_rows[: 2 * LW])[None]
    return (decoded, window_decoded)


def solution(mesh):
    fine = Mesh(mesh.devices.reshape(2, 2, 8, 8, 2), ("xh", "c", "z", "y", "xl"))
    segment = ("xh", "c")
    placed = (
        P(segment, LAT, None),
        P(),
        P(),
        P(),
        P(),
        P(segment, None, LAT),
        P(segment, None),
        P(),
    )
    return jax.shard_map(
        per_device,
        mesh=fine,
        in_specs=placed,
        out_specs=(P(segment, LAT, None), P(segment, LAT, None)),
        check_vma=False,
    )
```

```python
import math

import jax
import jax.numpy as jnp
from jax import lax
from jax.experimental import pallas as pl
from jax.experimental.pallas import tpu as pltpu
from jax.sharding import Mesh
from jax.sharding import PartitionSpec as P

HEAD_DIM = 64
LEV = 2
WIN_ROWS = 12
WIN_COLS = 6
WTOK = 144
FEAT = 144
LW = 7
PIECE = WIN_COLS * LEV * FEAT
PACK = 16
BF = jnp.bfloat16
F32 = jnp.float32
LAT = ("z", "y", "xl")
DOUBLING = (4, 2, 1)
OFFS = (0, 4, 2, 6, 1, 5, 3, 7)
MIB = 1 << 20

VMEM = pl.BlockSpec(memory_space=pltpu.VMEM)
SMEM = pl.BlockSpec(memory_space=pltpu.SMEM)
ANY = pl.BlockSpec(memory_space=pl.ANY)


def ring(value, axis, by):
    n = lax.axis_size(axis)
    return lax.ppermute(value, axis, [(i, (i + by) % n) for i in range(n)])


def swap(value, axis, bit):
    n = lax.axis_size(axis)
    return lax.ppermute(value, axis, [(i, i ^ bit) for i in range(n)])


def seventh(window):
    return lax.shift_right_logical(window * 147, 10)


def first_row(window):
    return WIN_ROWS * seventh(jnp.maximum(window, 0)) - WIN_ROWS // 2


def pack_kernel(where, bands, table, rows_ref, out_ref):
    column_of_bands, z = lax.rem(where[0], 16), where[1]
    starts, blocks = [], []
    total = jnp.int32(0)
    for far in range(bands.shape[0] // 16):
        def add(i, sums, base=16 * far):
            count = bands[base + i]
            return sums[0] + count, sums[1] + jnp.where(i < column_of_bands, count, 0)

        total, start = lax.fori_loop(0, 16, add, (total, total), unroll=4)
        starts.append(start)
        step = z ^ far
        place = (lax.rem(step, 2) * 4) | (step & 2) | lax.div(step, 4)
        blocks.append(place * 2 * LW)
    for shard in range(16):
        window = jnp.maximum(table[(z * 16 + shard) ^ where[4]], 0)
        first = first_row(window)
        block = jnp.int32(0)
        for start, at in zip(starts, blocks):
            row = start - first
            block = jnp.where((row >= -1) & (row < WIN_ROWS), at, block)
        column = block + window - LW * seventh(window)
        out_ref[2 * shard] = rows_ref[column]
        out_ref[2 * shard + 1] = rows_ref[LW + column]


def pick_kernel(where, bands, table, came_ref, out_ref):
    window = table[where[0] ^ where[4]]
    first = first_row(window)
    out_ref[...] = jnp.zeros_like(out_ref)
    count_rows = jnp.where(window >= 0, WIN_ROWS, 0)

    def band(i, row):
        count = bands[i]
        here = (row >= 0) & (row < count_rows)
        out_ref[jnp.where(here, row, WIN_ROWS)] = came_ref[2 * (i & 15)]
        here = (count > 1) & (row >= -1) & (row + 1 < count_rows)
        out_ref[jnp.where(here, row + 1, WIN_ROWS)] = came_ref[2 * (i & 15) + 1]
        return row + count

    lax.fori_loop(0, bands.shape[0], band, -first, unroll=8)


def unpick_kernel(where, bands, table, rows_ref, out_ref):
    first = first_row(table[where[0] ^ where[4]])

    def band(i, row):
        out_ref[2 * i] = rows_ref[jnp.clip(row, 0, WIN_ROWS - 1)]
        out_ref[2 * i + 1] = rows_ref[jnp.clip(row + 1, 0, WIN_ROWS - 1)]
        return row + bands[i]

    lax.fori_loop(0, bands.shape[0], band, -first, unroll=8)


def unpack_kernel(where, bands, table, came_ref, out_ref):
    mine = where[0]
    start = lax.fori_loop(
        0, bands.shape[0], lambda i, total: total + jnp.where(i < mine, bands[i], 0), jnp.int32(0), unroll=8
    )
    across = lax.div(start + WIN_ROWS // 2, WIN_ROWS)
    across_next = jnp.where(bands[mine] > 1, lax.div(start + 1 + WIN_ROWS // 2, WIN_ROWS), -1)
    out_ref[...] = jnp.zeros_like(out_ref)

    def shard(j, carry):
        held = table[j ^ where[4]]
        window = jnp.maximum(held, 0)
        line = jnp.where(held >= 0, seventh(window), -2)
        column = window - LW * seventh(window)
        out_ref[jnp.where(line == across, column, 2 * LW)] = came_ref[2 * j]
        out_ref[jnp.where(line == across_next, LW + column, 2 * LW)] = came_ref[2 * j + 1]
        return carry

    lax.fori_loop(0, table.shape[0], shard, 0, unroll=8)


def to_rows(tokens):
    rows = tokens.reshape(-1, PIECE)
    return jnp.pad(rows, ((0, 0), (0, PACK * 128 - PIECE))).reshape(-1, PACK, 128)


def from_rows(rows):
    return rows.reshape(-1, PACK * 128)[:, :PIECE].reshape(-1, FEAT)


def join_kernel(pos, *refs):
    out_ref, held, turned, sems, sent = refs[-5:]
    pieces = refs[:-5]
    half = len(pieces) // 2
    z, y = pos[1], pos[2]
    steps = (0, -1, -2, -3, 1, 2, 3, 4)

    def copies(side, index):
        ref = pieces[side * half + index]
        for sub in range(8):
            if side == 0:
                plane, line = lax.rem(z + steps[index] + 8, 8), y ^ OFFS[sub]
            else:
                plane, line = z ^ OFFS[sub], lax.rem(y + steps[index] + 8, 8)
            row = pl.multiple_of((plane * 8 + line) * 64, 64)
            yield pltpu.make_async_copy(
                ref.at[pl.ds(sub * 64, 64)], held.at[side, pl.ds(row, 64)], sems.at[side, index]
            )

    def turn(side, plane):
        columns = pl.ds(pl.multiple_of(plane * 512, 512), 512)
        here = (slice(512 * side, 512 * (side + 1)), columns)
        turned[here] = held[side, columns, :].T
        copy = pltpu.make_async_copy(turned.at[here], out_ref.at[here], sent)
        copy.start()
        return copy

    every = [[list(copies(side, index)) for index in range(half)] for side in range(2)]
    for side in range(2):
        for group in every[side]:
            for c in group:
                c.start()
    leaving = []
    for index in range(half):
        for c in every[0][index]:
            c.wait()
        leaving.append(turn(0, lax.rem(z + steps[index] + 8, 8)))
    for group in every[1]:
        for c in group:
            c.wait()
    for plane in range(8):
        leaving.append(turn(1, plane))
    for c in leaving:
        c.wait()


def gather_section(weight, pos, rows, gains, pack):
    mine = weight[0].T
    theirs, is_left = swap(mine, "xl", 1), lax.axis_index("xl") == 0
    pair = jnp.concatenate([jnp.where(is_left, mine, theirs), jnp.where(is_left, theirs, mine)])
    pair, gains = lax.optimization_barrier((pair, gains))
    a, b = pair[:, :512], pair[:, 512:]
    for bit in DOUBLING:
        a_far, b_far = swap(a, "y", bit), swap(b, "z", bit)
        a, b = jnp.concatenate([a, a_far]), jnp.concatenate([b, b_far])
    for bit in DOUBLING:
        rows = jnp.concatenate([rows, swap(rows, "z", bit)])
    a, b, rows = lax.optimization_barrier((a, b, rows))
    message = pack(rows)
    chains = [("z", 1), ("z", -1), ("y", 1), ("y", -1)]
    got = [[] for _ in chains]
    held = [a, a, b, b]
    for step in range(4):
        for n, (axis, by) in enumerate(chains):
            if step < 3 or by > 0:
                held[n] = ring(held[n], axis, by)
                got[n].append(held[n])
    *lasts, message = lax.optimization_barrier((*[g[-1] for g in got], message))
    for g, last in zip(got, lasts):
        g[-1] = last
    pieces = []
    for own, ahead, behind in ((a, got[0], got[1]), (b, got[2], got[3])):
        pieces += [own, *ahead[:3], *behind, ahead[3]]
    section = pl.pallas_call(
        join_kernel,
        out_shape=jax.ShapeDtypeStruct((1024, 4096), BF),
        in_specs=[SMEM] + [ANY] * len(pieces),
        out_specs=ANY,
        scratch_shapes=[
            pltpu.VMEM((2, 4096, 512), BF),
            pltpu.VMEM((1024, 4096), BF),
            pltpu.SemaphoreType.DMA((2, 8)),
            pltpu.SemaphoreType.DMA(()),
        ],
        compiler_params=pltpu.CompilerParams(vmem_limit_bytes=60 * MIB),
        cost_estimate=pl.CostEstimate(flops=10**10, bytes_accessed=3 << 23, transcendentals=0),
        name="join",
    )(pos, *pieces)
    return section, message, gains


def matmul_t(left, right):
    return lax.dot_general(left, right, (((1,), (1,)), ((), ())), preferred_element_type=F32)


def normed_of(wide, gain):
    scale = lax.rsqrt(jnp.mean(wide * wide, axis=-1, keepdims=True) + 1e-06)
    return (wide * scale * gain).astype(BF)


def other_level(value):
    half = WTOK // 2
    parts = [value[half * i : half * (i + 1)] for i in range(value.shape[0] // half)]
    return jnp.concatenate([parts[i ^ 1] for i in range(len(parts))], axis=0)


def column_block(hidden, gain, project):
    wide = hidden.astype(F32)
    normed = normed_of(wide, gain)
    query = project(normed, 0).astype(BF).astype(F32)
    keyed = project(normed, 1).astype(BF).astype(F32)
    product = query * (keyed - other_level(keyed))
    lane = lax.broadcasted_iota(jnp.int32, (1024, 128), 0)
    head = lax.broadcasted_iota(jnp.int32, (1024, 128), 1)
    of_head = (lax.div(lane, HEAD_DIM) == head).astype(BF)
    high = product.astype(BF)
    low = (product - high.astype(F32)).astype(BF)
    gap = (
        jnp.dot(high, of_head, preferred_element_type=F32)
        + jnp.dot(low, of_head, preferred_element_type=F32)
    ) * (1 / math.sqrt(HEAD_DIM))
    small = jnp.exp(-jnp.abs(gap))
    larger = 1.0 / (1.0 + small)
    smaller = small * larger
    own = jnp.where(gap >= 0, larger, smaller).astype(BF)
    far = jnp.where(gap >= 0, smaller, larger).astype(BF)
    valued = project(normed, 2).astype(BF).astype(F32)
    mixed = (matmul_t(own, of_head) * valued + matmul_t(far, of_head) * other_level(valued)).astype(BF)
    return (wide + project(mixed, 3)).astype(BF)


def window_block(hidden, gain, project, bias):
    wide = hidden.astype(F32)
    normed = normed_of(wide, gain)
    query = (project(normed, 0).astype(BF).astype(F32) * (1 / math.sqrt(HEAD_DIM))).astype(BF)
    keyed = project(normed, 1).astype(BF)
    valued = project(normed, 2).astype(BF)
    low = lax.broadcasted_iota(jnp.int32, (WTOK, 128), 1) < HEAD_DIM
    ones = jnp.ones((WTOK, 128), BF)
    slabs = []
    for slab in range(hidden.shape[0] // WTOK):
        here = slice(WTOK * slab, WTOK * (slab + 1))
        mixed = []
        for two in range(8):
            lanes = slice(128 * two, 128 * (two + 1))
            q2, k2 = query[here, lanes], keyed[here, lanes]
            v2 = jnp.concatenate([valued[here, lanes], ones], axis=1)
            outs = []
            for part in range(2):
                q1 = jnp.where(low if part == 0 else ~low, q2, jnp.zeros_like(q2))
                scores = matmul_t(q1, k2) + bias
                top = jnp.max(scores, axis=-1, keepdims=True)
                grown = jnp.exp(scores - top).astype(BF)
                summed = jnp.dot(grown, v2, preferred_element_type=F32)
                outs.append(summed[:, :128] / summed[:, 128:])
            mixed.append(jnp.where(low, outs[0], outs[1]).astype(BF))
        slabs.append(jnp.concatenate(mixed, axis=1))
    mixed = jnp.concatenate(slabs, axis=0)
    return (wide + project(mixed, 3)).astype(BF)


def projections(pos, own_ref, other_ref, weights, sems):
    core = pos[3]

    def load(source, section):
        for part in range(4):
            columns = pl.ds(1024 * part, 1024)
            pltpu.make_async_copy(
                source.at[:, columns], weights.at[section, :, columns], sems.at[section, part]
            ).start()

    @pl.when(core == 0)
    def _():
        load(own_ref, 0)
        load(other_ref, 1)

    @pl.when(core == 1)
    def _():
        load(other_ref, 0)
        load(own_ref, 1)

    def of_section(section):
        def project(left, part):
            columns = pl.ds(1024 * part, 1024)
            pltpu.make_async_copy(
                own_ref.at[:, columns], weights.at[section, :, columns], sems.at[section, part]
            ).wait()
            right = weights[section, :, 1024 * part : 1024 * (part + 1)]
            return jnp.dot(left, right, preferred_element_type=F32)

        return project

    return of_section(0), of_section(1)


def inside(pos, bands, table, token):
    window = table[pos[0] ^ pos[4]]
    row = first_row(window) + lax.rem(lax.div(token, WIN_COLS), WIN_ROWS)
    return (window >= 0) & (row >= 0) & (row < 3 * bands.shape[0] // 2)


def key_bias(pos, bands, table):
    token = lax.broadcasted_iota(jnp.int32, (1, WTOK), 1)
    return jnp.where(inside(pos, bands, table, token), 0.0, -1e30)


def early_kernel(
    pos, bands, table, raw_ref, embed_ref, level_ref, gain_ref, own_ref, other_ref,
    hidden_ref, weights, sems,
):
    first, second = projections(pos, own_ref, other_ref, weights, sems)
    to_token = lax.broadcasted_iota(jnp.int32, (WTOK, WTOK), 0)
    from_token = lax.broadcasted_iota(jnp.int32, (WTOK, WTOK), 1)
    half = WTOK // 2
    to_window = (lax.div(to_token, half) == lax.rem(from_token, LEV)) & (
        lax.rem(to_token, half) == lax.div(from_token, LEV)
    )
    raw = jnp.dot(to_window.astype(BF), raw_ref[...], preferred_element_type=F32).astype(BF)
    upper = lax.broadcasted_iota(jnp.int32, (WTOK, 1), 0) < half
    level_rows = jnp.where(upper, level_ref[0:1].astype(F32), level_ref[1:2].astype(F32))
    embedded = (jnp.dot(raw, embed_ref[...], preferred_element_type=F32) + level_rows).astype(BF)
    hidden = column_block(embedded, gain_ref[0:1], first)
    hidden_ref[...] = window_block(hidden, gain_ref[1:2], second, key_bias(pos, bands, table))


def late_kernel(
    pos, bands, table, came_ref, came_too_ref, gain_ref, head_ref, own_ref, other_ref,
    give_ref, out_ref, rows_ref, weights, sems,
):
    first, second = projections(pos, own_ref, other_ref, weights, sems)
    start = jnp.concatenate([came_ref[...], came_too_ref[...]], axis=0)
    hidden = window_block(start, gain_ref[0:1], first, key_bias(pos, bands, table))
    hidden = column_block(hidden, gain_ref[1:2], second)
    result = jnp.dot(hidden, head_ref[...], preferred_element_type=F32)
    keep = inside(pos, bands, table, lax.broadcasted_iota(jnp.int32, (WTOK, 1), 0))
    to_token = lax.broadcasted_iota(jnp.int32, (WTOK, WTOK), 0)
    from_token = lax.broadcasted_iota(jnp.int32, (WTOK, WTOK), 1)
    half = WTOK // 2
    from_window = (lax.rem(to_token, LEV) == lax.div(from_token, half)) & (
        lax.div(to_token, LEV) == lax.rem(from_token, half)
    )
    from_window = from_window.astype(BF)
    for slab in range(2):
        out = jnp.where(keep, result[WTOK * slab : WTOK * (slab + 1)], 0.0).astype(BF)
        rows = jnp.dot(from_window, out, preferred_element_type=F32).astype(BF)
        if slab == 0:
            give_ref[0], give_ref[1] = out, rows
        else:
            out_ref[...], rows_ref[...] = out, rows


def sections_call(body, shapes, scalars, values, own, other, name):
    return pl.pallas_call(
        body,
        out_shape=tuple(jax.ShapeDtypeStruct(shape, BF) for shape in shapes),
        in_specs=[SMEM] * len(scalars) + [VMEM] * len(values) + [ANY] * 2,
        out_specs=(VMEM,) * len(shapes),
        scratch_shapes=[
            pltpu.VMEM((2, 1024, 4096), BF),
            pltpu.SemaphoreType.DMA((2, 4)),
        ],
        compiler_params=pltpu.CompilerParams(vmem_limit_bytes=60 * MIB),
        name=name,
    )(*scalars, *values, own, other)


def small_call(body, out_rows, scalars, value, name):
    return pl.pallas_call(
        body,
        out_shape=jax.ShapeDtypeStruct((out_rows, PACK, 128), BF),
        in_specs=[SMEM] * len(scalars) + [VMEM],
        out_specs=VMEM,
        name=name,
    )(*scalars, value)


def crossed(value, sources):
    return lax.ppermute(value, ("xh", "xl"), [(x, 3 - x) for x in sources])


def per_device(
    fields, band_rows, window_table, level_embed, embed_weight, attn_weight, norm_gain, head_weight
):
    late, core = lax.axis_index("xh"), lax.axis_index("c")
    is_late = late == 1
    pos = jnp.stack([lax.axis_index(LAT), lax.axis_index("z"), lax.axis_index("y"), core, late])
    lat_count = band_rows.shape[0]
    width = embed_weight.shape[1]
    scalars = (pos, band_rows, window_table)

    gains = lax.all_gather(norm_gain, "c", axis=0, tiled=True)
    own, message, gains = gather_section(
        attn_weight,
        pos,
        to_rows(fields[0]),
        gains,
        lambda rows: small_call(pack_kernel, 32, scalars, rows, "pack"),
    )
    arrived = lax.all_to_all(message, ("y", "xl"), 0, 0, tiled=True)
    other = swap(own, "c", 1)
    raw_rows = small_call(pick_kernel, WIN_ROWS + 1, scalars, arrived, "pick")
    own_raw = from_rows(raw_rows[:WIN_ROWS])
    far_raw = crossed(own_raw, (2, 3))

    def early(raw):
        [hidden] = sections_call(
            early_kernel,
            [(WTOK, width)],
            scalars,
            (raw, embed_weight, level_embed, gains),
            own,
            other,
            "early",
        )
        return hidden

    too = crossed(early(far_raw), (0, 1))
    came = [crossed(early(own_raw), (0, 1)), too]
    given, out, rows = sections_call(
        late_kernel,
        [(2, WTOK, FEAT), (WTOK, FEAT), (WTOK, FEAT)],
        scalars,
        (*came, gains, head_weight),
        own,
        other,
        "late",
    )
    taken = crossed(given, (2, 3))
    own_rows = jnp.where(is_late, rows, taken[1])
    reply = small_call(unpick_kernel, 2 * lat_count, scalars, to_rows(own_rows), "unpick")
    came_back = lax.all_to_all(reply, LAT, 0, 0, tiled=True)
    window_decoded = jnp.where(is_late, swap(out, "xl", 1), taken[0])[None]
    decoded_rows = small_call(unpack_kernel, 2 * LW + 1, scalars, came_back, "unpack")
    decoded = from_rows(decoded_rows[: 2 * LW])[None]
    return (decoded, window_decoded)


def solution(mesh):
    fine = Mesh(mesh.devices.reshape(2, 2, 8, 8, 2), ("xh", "c", "z", "y", "xl"))
    segment = ("xh", "c")
    placed = (
        P(segment, LAT, None),
        P(),
        P(),
        P(),
        P(),
        P(segment, None, LAT),
        P(segment, None),
        P(),
    )
    return jax.shard_map(
        per_device,
        mesh=fine,
        in_specs=placed,
        out_specs=(P(segment, LAT, None), P(segment, LAT, None)),
        check_vma=False,
    )
```

```python
import math

import jax
import jax.numpy as jnp
from jax import lax
from jax.experimental import pallas as pl
from jax.experimental.pallas import tpu as pltpu
from jax.sharding import Mesh
from jax.sharding import PartitionSpec as P

HEAD_DIM = 64
LEV = 2
WIN_ROWS = 12
WIN_COLS = 6
WTOK = 144
FEAT = 144
LW = 7
PIECE = WIN_COLS * LEV * FEAT
PACK = 16
BF = jnp.bfloat16
F32 = jnp.float32
LAT = ("z", "y", "xl")
DOUBLING = (4, 2, 1)
OFFS = (0, 4, 2, 6, 1, 5, 3, 7)
MIB = 1 << 20

VMEM = pl.BlockSpec(memory_space=pltpu.VMEM)
SMEM = pl.BlockSpec(memory_space=pltpu.SMEM)
ANY = pl.BlockSpec(memory_space=pl.ANY)


def ring(value, axis, by):
    n = lax.axis_size(axis)
    return lax.ppermute(value, axis, [(i, (i + by) % n) for i in range(n)])


def swap(value, axis, bit):
    n = lax.axis_size(axis)
    return lax.ppermute(value, axis, [(i, i ^ bit) for i in range(n)])


def seventh(window):
    return lax.shift_right_logical(window * 147, 10)


def first_row(window):
    return WIN_ROWS * seventh(jnp.maximum(window, 0)) - WIN_ROWS // 2


def pack_kernel(where, bands, table, rows_ref, out_ref):
    column_of_bands, z = lax.rem(where[0], 16), where[1]
    starts, blocks = [], []
    total = jnp.int32(0)
    for far in range(bands.shape[0] // 16):
        def add(i, sums, base=16 * far):
            count = bands[base + i]
            return sums[0] + count, sums[1] + jnp.where(i < column_of_bands, count, 0)

        total, start = lax.fori_loop(0, 16, add, (total, total), unroll=4)
        starts.append(start)
        step = z ^ far
        place = (lax.rem(step, 2) * 4) | (step & 2) | lax.div(step, 4)
        blocks.append(place * 2 * LW)
    for shard in range(16):
        window = jnp.maximum(table[(z * 16 + shard) ^ where[4]], 0)
        first = first_row(window)
        block = jnp.int32(0)
        for start, at in zip(starts, blocks):
            row = start - first
            block = jnp.where((row >= -1) & (row < WIN_ROWS), at, block)
        column = block + window - LW * seventh(window)
        out_ref[2 * shard] = rows_ref[column]
        out_ref[2 * shard + 1] = rows_ref[LW + column]


def pick_kernel(where, bands, table, came_ref, out_ref):
    window = table[where[0] ^ where[4]]
    first = first_row(window)
    out_ref[...] = jnp.zeros_like(out_ref)
    count_rows = jnp.where(window >= 0, WIN_ROWS, 0)

    def band(i, row):
        count = bands[i]
        here = (row >= 0) & (row < count_rows)
        out_ref[jnp.where(here, row, WIN_ROWS)] = came_ref[2 * (i & 15)]
        here = (count > 1) & (row >= -1) & (row + 1 < count_rows)
        out_ref[jnp.where(here, row + 1, WIN_ROWS)] = came_ref[2 * (i & 15) + 1]
        return row + count

    lax.fori_loop(0, bands.shape[0], band, -first, unroll=8)


def unpick_kernel(where, bands, table, rows_ref, out_ref):
    first = first_row(table[where[0] ^ where[4]])

    def band(i, row):
        out_ref[2 * i] = rows_ref[jnp.clip(row, 0, WIN_ROWS - 1)]
        out_ref[2 * i + 1] = rows_ref[jnp.clip(row + 1, 0, WIN_ROWS - 1)]
        return row + bands[i]

    lax.fori_loop(0, bands.shape[0], band, -first, unroll=8)


def unpack_kernel(where, bands, table, came_ref, out_ref):
    mine = where[0]
    start = lax.fori_loop(
        0, bands.shape[0], lambda i, total: total + jnp.where(i < mine, bands[i], 0), jnp.int32(0), unroll=8
    )
    across = lax.div(start + WIN_ROWS // 2, WIN_ROWS)
    across_next = jnp.where(bands[mine] > 1, lax.div(start + 1 + WIN_ROWS // 2, WIN_ROWS), -1)
    out_ref[...] = jnp.zeros_like(out_ref)

    def shard(j, carry):
        held = table[j ^ where[4]]
        window = jnp.maximum(held, 0)
        line = jnp.where(held >= 0, seventh(window), -2)
        column = window - LW * seventh(window)
        out_ref[jnp.where(line == across, column, 2 * LW)] = came_ref[2 * j]
        out_ref[jnp.where(line == across_next, LW + column, 2 * LW)] = came_ref[2 * j + 1]
        return carry

    lax.fori_loop(0, table.shape[0], shard, 0, unroll=8)


def to_rows(tokens):
    rows = tokens.reshape(-1, PIECE)
    return jnp.pad(rows, ((0, 0), (0, PACK * 128 - PIECE))).reshape(-1, PACK, 128)


def from_rows(rows):
    return rows.reshape(-1, PACK * 128)[:, :PIECE].reshape(-1, FEAT)


def join_kernel(pos, *refs):
    out_ref, held, turned, sems, sent = refs[-5:]
    pieces = refs[:-5]
    half = len(pieces) // 2
    z, y = pos[1], pos[2]
    steps = (0, -1, -2, -3, 1, 2, 3, 4, 4)

    def copies(side, index):
        ref = pieces[side * half + index]
        subs = range(8) if index < 7 else (range(4) if index == 7 else range(4, 8))
        for slot, sub in enumerate(subs):
            if side == 0:
                plane, line = lax.rem(z + steps[index] + 8, 8), y ^ OFFS[sub]
            else:
                plane, line = z ^ OFFS[sub], lax.rem(y + steps[index] + 8, 8)
            row = pl.multiple_of((plane * 8 + line) * 64, 64)
            yield pltpu.make_async_copy(
                ref.at[pl.ds(slot * 64, 64)], held.at[side, pl.ds(row, 64)], sems.at[side, index]
            )

    def turn(side, plane):
        columns = pl.ds(pl.multiple_of(plane * 512, 512), 512)
        here = (slice(512 * side, 512 * (side + 1)), columns)
        turned[here] = held[side, columns, :].T
        copy = pltpu.make_async_copy(turned.at[here], out_ref.at[here], sent)
        copy.start()
        return copy

    every = [[list(copies(side, index)) for index in range(half)] for side in range(2)]
    for side in range(2):
        for group in every[side]:
            for c in group:
                c.start()
    leaving = []
    for index in range(half):
        for c in every[0][index]:
            c.wait()
        if index != 7:
            leaving.append(turn(0, lax.rem(z + steps[index] + 8, 8)))
    for group in every[1]:
        for c in group:
            c.wait()
    for plane in range(8):
        leaving.append(turn(1, plane))
    for c in leaving:
        c.wait()


def gather_section(weight, pos, rows, gains, pack):
    mine = weight[0].T
    theirs, is_left = swap(mine, "xl", 1), lax.axis_index("xl") == 0
    pair = jnp.concatenate([jnp.where(is_left, mine, theirs), jnp.where(is_left, theirs, mine)])
    pair, gains = lax.optimization_barrier((pair, gains))
    a, b = pair[:, :512], pair[:, 512:]
    for bit in DOUBLING:
        a_far, b_far = swap(a, "y", bit), swap(b, "z", bit)
        a, b = jnp.concatenate([a, a_far]), jnp.concatenate([b, b_far])
    for bit in DOUBLING:
        rows = jnp.concatenate([rows, swap(rows, "z", bit)])
    a, b, rows = lax.optimization_barrier((a, b, rows))
    message = pack(rows)
    chains = [("z", 1), ("z", -1), ("y", 1), ("y", -1)]
    got = [[] for _ in chains]
    held = [a, a, b, b]
    for step in range(4):
        for n, (axis, by) in enumerate(chains):
            value = held[n]
            if step == 3:
                value = value[:256] if by > 0 else value[256:]
            held[n] = ring(value, axis, by)
            got[n].append(held[n])
    *lasts, message = lax.optimization_barrier((*[g[-1] for g in got], message))
    for g, last in zip(got, lasts):
        g[-1] = last
    pieces = []
    for own, ahead, behind in ((a, got[0], got[1]), (b, got[2], got[3])):
        pieces += [own, *ahead[:3], *behind[:3], ahead[3], behind[3]]
    section = pl.pallas_call(
        join_kernel,
        out_shape=jax.ShapeDtypeStruct((1024, 4096), BF),
        in_specs=[SMEM] + [ANY] * len(pieces),
        out_specs=ANY,
        scratch_shapes=[
            pltpu.VMEM((2, 4096, 512), BF),
            pltpu.VMEM((1024, 4096), BF),
            pltpu.SemaphoreType.DMA((2, 9)),
            pltpu.SemaphoreType.DMA(()),
        ],
        compiler_params=pltpu.CompilerParams(vmem_limit_bytes=60 * MIB),
        cost_estimate=pl.CostEstimate(flops=10**10, bytes_accessed=3 << 23, transcendentals=0),
        name="join",
    )(pos, *pieces)
    return section, message, gains


def matmul_t(left, right):
    return lax.dot_general(left, right, (((1,), (1,)), ((), ())), preferred_element_type=F32)


def normed_of(wide, gain):
    scale = lax.rsqrt(jnp.mean(wide * wide, axis=-1, keepdims=True) + 1e-06)
    return (wide * scale * gain).astype(BF)


def other_level(value):
    half = WTOK // 2
    parts = [value[half * i : half * (i + 1)] for i in range(value.shape[0] // half)]
    return jnp.concatenate([parts[i ^ 1] for i in range(len(parts))], axis=0)


def column_block(hidden, gain, project):
    wide = hidden.astype(F32)
    normed = normed_of(wide, gain)
    query = project(normed, 0).astype(BF).astype(F32)
    keyed = project(normed, 1).astype(BF).astype(F32)
    product = query * (keyed - other_level(keyed))
    lane = lax.broadcasted_iota(jnp.int32, (1024, 128), 0)
    head = lax.broadcasted_iota(jnp.int32, (1024, 128), 1)
    of_head = (lax.div(lane, HEAD_DIM) == head).astype(BF)
    high = product.astype(BF)
    low = (product - high.astype(F32)).astype(BF)
    gap = (
        jnp.dot(high, of_head, preferred_element_type=F32)
        + jnp.dot(low, of_head, preferred_element_type=F32)
    ) * (1 / math.sqrt(HEAD_DIM))
    small = jnp.exp(-jnp.abs(gap))
    larger = 1.0 / (1.0 + small)
    smaller = small * larger
    own = jnp.where(gap >= 0, larger, smaller).astype(BF)
    far = jnp.where(gap >= 0, smaller, larger).astype(BF)
    valued = project(normed, 2).astype(BF).astype(F32)
    mixed = (matmul_t(own, of_head) * valued + matmul_t(far, of_head) * other_level(valued)).astype(BF)
    return (wide + project(mixed, 3)).astype(BF)


def window_block(hidden, gain, project, bias):
    wide = hidden.astype(F32)
    normed = normed_of(wide, gain)
    query = (project(normed, 0).astype(BF).astype(F32) * (1 / math.sqrt(HEAD_DIM))).astype(BF)
    keyed = project(normed, 1).astype(BF)
    valued = project(normed, 2).astype(BF)
    low = lax.broadcasted_iota(jnp.int32, (WTOK, 128), 1) < HEAD_DIM
    ones = jnp.ones((WTOK, 128), BF)
    slabs = []
    for slab in range(hidden.shape[0] // WTOK):
        here = slice(WTOK * slab, WTOK * (slab + 1))
        mixed = []
        for two in range(8):
            lanes = slice(128 * two, 128 * (two + 1))
            q2, k2 = query[here, lanes], keyed[here, lanes]
            v2 = jnp.concatenate([valued[here, lanes], ones], axis=1)
            outs = []
            for part in range(2):
                q1 = jnp.where(low if part == 0 else ~low, q2, jnp.zeros_like(q2))
                scores = matmul_t(q1, k2) + bias
                top = jnp.max(scores, axis=-1, keepdims=True)
                grown = jnp.exp(scores - top).astype(BF)
                summed = jnp.dot(grown, v2, preferred_element_type=F32)
                outs.append(summed[:, :128] / summed[:, 128:])
            mixed.append(jnp.where(low, outs[0], outs[1]).astype(BF))
        slabs.append(jnp.concatenate(mixed, axis=1))
    mixed = jnp.concatenate(slabs, axis=0)
    return (wide + project(mixed, 3)).astype(BF)


def projections(pos, own_ref, other_ref, weights, sems):
    core = pos[3]

    def load(source, section):
        for part in range(4):
            columns = pl.ds(1024 * part, 1024)
            pltpu.make_async_copy(
                source.at[:, columns], weights.at[section, :, columns], sems.at[section, part]
            ).start()

    @pl.when(core == 0)
    def _():
        load(own_ref, 0)
        load(other_ref, 1)

    @pl.when(core == 1)
    def _():
        load(other_ref, 0)
        load(own_ref, 1)

    def of_section(section):
        def project(left, part):
            columns = pl.ds(1024 * part, 1024)
            pltpu.make_async_copy(
                own_ref.at[:, columns], weights.at[section, :, columns], sems.at[section, part]
            ).wait()
            right = weights[section, :, 1024 * part : 1024 * (part + 1)]
            return jnp.dot(left, right, preferred_element_type=F32)

        return project

    return of_section(0), of_section(1)


def inside(pos, bands, table, token):
    window = table[pos[0] ^ pos[4]]
    row = first_row(window) + lax.rem(lax.div(token, WIN_COLS), WIN_ROWS)
    return (window >= 0) & (row >= 0) & (row < 3 * bands.shape[0] // 2)


def key_bias(pos, bands, table):
    token = lax.broadcasted_iota(jnp.int32, (1, WTOK), 1)
    return jnp.where(inside(pos, bands, table, token), 0.0, -1e30)


def early_kernel(
    pos, bands, table, raw_ref, embed_ref, level_ref, gain_ref, own_ref, other_ref,
    hidden_ref, weights, sems,
):
    first, second = projections(pos, own_ref, other_ref, weights, sems)
    to_token = lax.broadcasted_iota(jnp.int32, (WTOK, WTOK), 0)
    from_token = lax.broadcasted_iota(jnp.int32, (WTOK, WTOK), 1)
    half = WTOK // 2
    to_window = (lax.div(to_token, half) == lax.rem(from_token, LEV)) & (
        lax.rem(to_token, half) == lax.div(from_token, LEV)
    )
    raw = jnp.dot(to_window.astype(BF), raw_ref[...], preferred_element_type=F32).astype(BF)
    upper = lax.broadcasted_iota(jnp.int32, (WTOK, 1), 0) < half
    level_rows = jnp.where(upper, level_ref[0:1].astype(F32), level_ref[1:2].astype(F32))
    embedded = (jnp.dot(raw, embed_ref[...], preferred_element_type=F32) + level_rows).astype(BF)
    hidden = column_block(embedded, gain_ref[0:1], first)
    hidden_ref[...] = window_block(hidden, gain_ref[1:2], second, key_bias(pos, bands, table))


def late_kernel(
    pos, bands, table, came_ref, came_too_ref, gain_ref, head_ref, own_ref, other_ref,
    give_ref, out_ref, rows_ref, weights, sems,
):
    first, second = projections(pos, own_ref, other_ref, weights, sems)
    start = jnp.concatenate([came_ref[...], came_too_ref[...]], axis=0)
    hidden = window_block(start, gain_ref[0:1], first, key_bias(pos, bands, table))
    hidden = column_block(hidden, gain_ref[1:2], second)
    result = jnp.dot(hidden, head_ref[...], preferred_element_type=F32)
    keep = inside(pos, bands, table, lax.broadcasted_iota(jnp.int32, (WTOK, 1), 0))
    to_token = lax.broadcasted_iota(jnp.int32, (WTOK, WTOK), 0)
    from_token = lax.broadcasted_iota(jnp.int32, (WTOK, WTOK), 1)
    half = WTOK // 2
    from_window = (lax.rem(to_token, LEV) == lax.div(from_token, half)) & (
        lax.div(to_token, LEV) == lax.rem(from_token, half)
    )
    from_window = from_window.astype(BF)
    for slab in range(2):
        out = jnp.where(keep, result[WTOK * slab : WTOK * (slab + 1)], 0.0).astype(BF)
        rows = jnp.dot(from_window, out, preferred_element_type=F32).astype(BF)
        if slab == 0:
            give_ref[0], give_ref[1] = out, rows
        else:
            out_ref[...], rows_ref[...] = out, rows


def sections_call(body, shapes, scalars, values, own, other, name):
    return pl.pallas_call(
        body,
        out_shape=tuple(jax.ShapeDtypeStruct(shape, BF) for shape in shapes),
        in_specs=[SMEM] * len(scalars) + [VMEM] * len(values) + [ANY] * 2,
        out_specs=(VMEM,) * len(shapes),
        scratch_shapes=[
            pltpu.VMEM((2, 1024, 4096), BF),
            pltpu.SemaphoreType.DMA((2, 4)),
        ],
        compiler_params=pltpu.CompilerParams(vmem_limit_bytes=60 * MIB),
        name=name,
    )(*scalars, *values, own, other)


def small_call(body, out_rows, scalars, value, name):
    return pl.pallas_call(
        body,
        out_shape=jax.ShapeDtypeStruct((out_rows, PACK, 128), BF),
        in_specs=[SMEM] * len(scalars) + [VMEM],
        out_specs=VMEM,
        name=name,
    )(*scalars, value)


def crossed(value, sources):
    return lax.ppermute(value, ("xh", "xl"), [(x, 3 - x) for x in sources])


def per_device(
    fields, band_rows, window_table, level_embed, embed_weight, attn_weight, norm_gain, head_weight
):
    late, core = lax.axis_index("xh"), lax.axis_index("c")
    is_late = late == 1
    pos = jnp.stack([lax.axis_index(LAT), lax.axis_index("z"), lax.axis_index("y"), core, late])
    lat_count = band_rows.shape[0]
    width = embed_weight.shape[1]
    scalars = (pos, band_rows, window_table)

    gains = lax.all_gather(norm_gain, "c", axis=0, tiled=True)
    own, message, gains = gather_section(
        attn_weight,
        pos,
        to_rows(fields[0]),
        gains,
        lambda rows: small_call(pack_kernel, 32, scalars, rows, "pack"),
    )
    arrived = lax.all_to_all(message, ("y", "xl"), 0, 0, tiled=True)
    other = swap(own, "c", 1)
    raw_rows = small_call(pick_kernel, WIN_ROWS + 1, scalars, arrived, "pick")
    own_raw = from_rows(raw_rows[:WIN_ROWS])
    far_raw = crossed(own_raw, (2, 3))

    def early(raw):
        [hidden] = sections_call(
            early_kernel,
            [(WTOK, width)],
            scalars,
            (raw, embed_weight, level_embed, gains),
            own,
            other,
            "early",
        )
        return hidden

    too = crossed(early(far_raw), (0, 1))
    came = [crossed(early(own_raw), (0, 1)), too]
    given, out, rows = sections_call(
        late_kernel,
        [(2, WTOK, FEAT), (WTOK, FEAT), (WTOK, FEAT)],
        scalars,
        (*came, gains, head_weight),
        own,
        other,
        "late",
    )
    taken = crossed(given, (2, 3))
    own_rows = jnp.where(is_late, rows, taken[1])
    reply = small_call(unpick_kernel, 2 * lat_count, scalars, to_rows(own_rows), "unpick")
    came_back = lax.all_to_all(reply, LAT, 0, 0, tiled=True)
    window_decoded = jnp.where(is_late, swap(out, "xl", 1), taken[0])[None]
    decoded_rows = small_call(unpack_kernel, 2 * LW + 1, scalars, came_back, "unpack")
    decoded = from_rows(decoded_rows[: 2 * LW])[None]
    return (decoded, window_decoded)


def solution(mesh):
    fine = Mesh(mesh.devices.reshape(2, 2, 8, 8, 2), ("xh", "c", "z", "y", "xl"))
    segment = ("xh", "c")
    placed = (
        P(segment, LAT, None),
        P(),
        P(),
        P(),
        P(),
        P(segment, None, LAT),
        P(segment, None),
        P(),
    )
    return jax.shard_map(
        per_device,
        mesh=fine,
        in_specs=placed,
        out_specs=(P(segment, LAT, None), P(segment, LAT, None)),
        check_vma=False,
    )
```
